512 devices in a mesh: gx: 16 (over x, y), gy: 32 (over z, core).
Axes of the slice: x: 4, y: 4, z: 16, core: 2. Of those that a mesh axis runs over, the one named last changes fastest.
Arguments:
- start_field: float32 [256, 512, 256], P('gx', 'gy'), may hold values from -3 to 3
- dielectric: float32 [256, 512, 256], P('gx', 'gy'), may hold values from 1 to 10
- ion_weight: float32 [256, 512, 256], P('gx', 'gy'), may hold values from 0.1 to 3
- source: float32 [256, 512, 256], P('gx', 'gy'), may hold values from -12 to 12
Outputs:
- relaxed_field: float32 [256, 512, 256], P('gx', 'gy')
- residual_norm: float32 [], replicated
The draws below stay inside these ranges and needn't reach their ends.
All inputs are finite; a program needn't handle non-finite values.
Results may differ from the reference program's by a relative error of at most 0.00002.
Values sent between devices are 32-bit elements; how exact they have to be, the bound alone decides.
No kernel may reach another device: no remote copies, remote signals or barrier semaphores. Data moves between devices by JAX's collectives and lax.ppermute only.
A program may use at most 128 MiB of HBM per device.

```python
import math
import jax
import jax.numpy as jnp

NZ = 256
PRE = 2
POST = 2
COARSE = 4
NX = 256
NY = 512


def block_levels(key, dims, shards, least, high):
    gain, own = 1.0, jax.random.fold_in(key, 6)
    for axis_at, shards_of in shards:
        heights = jnp.exp(jax.random.uniform(jax.random.fold_in(own, axis_at), (shards_of,), jnp.float32, least / len(shards), high / len(shards)))
        gain = gain * jnp.repeat(heights, dims[axis_at] // shards_of).reshape([-1 if axis == axis_at else 1 for axis in range(len(dims))])
    return gain


def gaussian(rng, extent, scale, limit, split=(), held_as=jnp.bfloat16):
    array = scale * jax.random.normal(rng, extent, jnp.float32)
    if split:
        array = array * block_levels(rng, extent, split, -0.22, 0.18)
    return jnp.clip(array, -limit, limit).astype(held_as)


def setup_inputs(seed: int = 0) -> dict:
    key_of = jax.random.split(jax.random.key(seed), 5)
    return {
        "start_field": gaussian(key_of[0], (NX, NY, NZ), 0.5, 3.0, ((0, 16), (1, 32)), jnp.float32),
        "dielectric": jnp.clip(jnp.exp(math.log(10.0) - 2.3025851 * jax.random.uniform(key_of[1], (NX, NY, NZ), jnp.float32) ** block_levels(key_of[1], (NX, NY, NZ), ((0, 16), (1, 32)), -0.2, 0.2)), 1.0, 10.0),
        "ion_weight": jnp.clip(jnp.exp(math.log(3.0) - 3.4011974 * jax.random.uniform(key_of[2], (NX, NY, NZ), jnp.float32) ** block_levels(key_of[2], (NX, NY, NZ), ((0, 16), (1, 32)), -0.2, 0.2)), 0.1, 3.0),
        "source": gaussian(key_of[3], (NX, NY, NZ), 2.0, 12.0, ((0, 16), (1, 32)), jnp.float32),
    }


OMEGA = 0.8
NEIGHBOURS = ((slice(2, None), slice(1, -1), slice(1, -1)), (slice(0, -2), slice(1, -1), slice(1, -1)), (slice(1, -1), slice(2, None), slice(1, -1)), (slice(1, -1), slice(0, -2), slice(1, -1)), (slice(1, -1), slice(1, -1), slice(2, None)), (slice(1, -1), slice(1, -1), slice(0, -2)))

def relax_cells(padded, statics, level_scale):
    permit = jnp.pad(statics[0], ((0, 0), (0, 0), (1, 1)))
    field = jnp.pad(padded, ((0, 0), (0, 0), (1, 1)))
    centre = field[1:-1, 1:-1, 1:-1]
    own_permit = permit[1:-1, 1:-1, 1:-1]
    flux = jnp.zeros_like(centre)
    faces = jnp.zeros_like(centre)
    for view in NEIGHBOURS:
        face = 0.5 * (own_permit + permit[view])
        flux = flux + face * (centre - field[view])
        faces = faces + face
    ion = statics[1][1:-1, 1:-1, :]
    load = statics[2][1:-1, 1:-1, :]
    defect = load - (level_scale * flux + ion * jnp.sinh(centre))
    slope = level_scale * faces + ion * jnp.cosh(centre)
    return (centre, defect, slope)

def restrict_cells(values):
    sx, sy, sz = values.shape
    return values.reshape(sx // 2, 2, sy // 2, 2, sz // 2, 2).mean(axis=(1, 3, 5))

def prolong_cells(values):
    return jnp.repeat(jnp.repeat(jnp.repeat(values, 2, 0), 2, 1), 2, 2)

def pad_field(field):
    return jnp.pad(field, ((1, 1), (1, 1), (0, 0)))

def pad_stack(stack):
    return jnp.pad(stack, ((0, 0), (1, 1), (1, 1), (0, 0)))

def smooth_level(field, statics, level_scale, sweeps):
    for sweep_index in range(sweeps):
        centre, defect, slope = relax_cells(pad_field(field), statics, level_scale)
        field = centre + OMEGA * defect / slope
    return field

def defect_of(field, statics, level_scale):
    return relax_cells(pad_field(field), statics, level_scale)[1]

def level_load(permit, ion, field, restricted, level_scale):
    zeros_field = jnp.zeros_like(field)
    loadless = pad_stack(jnp.stack([permit, ion, zeros_field]))
    return restricted + defect_of(field, loadless, level_scale)

def reference(start_field, dielectric, ion_weight, source):
    statics_zero = pad_stack(jnp.stack([dielectric, ion_weight, source]))
    field_zero = smooth_level(start_field, statics_zero, 1.0, PRE)
    defect_zero = defect_of(field_zero, statics_zero, 1.0)
    permit_one = restrict_cells(dielectric)
    ion_one = restrict_cells(ion_weight)
    start_one = restrict_cells(field_zero)
    load_one = level_load(permit_one, ion_one, start_one, restrict_cells(defect_zero), 0.25)
    statics_one = pad_stack(jnp.stack([permit_one, ion_one, load_one]))
    field_one = smooth_level(start_one, statics_one, 0.25, PRE)
    defect_one = defect_of(field_one, statics_one, 0.25)
    permit_two = restrict_cells(permit_one)
    ion_two = restrict_cells(ion_one)
    start_two = restrict_cells(field_one)
    load_two = level_load(permit_two, ion_two, start_two, restrict_cells(defect_one), 0.0625)
    statics_two = pad_stack(jnp.stack([permit_two, ion_two, load_two]))
    field_two = smooth_level(start_two, statics_two, 0.0625, COARSE)
    field_one = field_one + prolong_cells(field_two - start_two)
    field_one = smooth_level(field_one, statics_one, 0.25, POST)
    relaxed = field_zero + prolong_cells(field_one - start_one)
    relaxed = smooth_level(relaxed, statics_zero, 1.0, POST)
    final_defect = defect_of(relaxed, statics_zero, 1.0)
    total = jnp.sum(final_defect * final_defect)
    return (relaxed, jnp.sqrt(total / final_defect.size))
```

```python
import functools

import jax
import jax.numpy as jnp
from jax import lax
from jax.experimental import pallas as pl
from jax.experimental.pallas import tpu as pltpu
from jax.sharding import PartitionSpec as P

OMEGA = 0.8
LN2 = 0.6931471805599453
F32 = jnp.float32
HIGHEST = lax.Precision.HIGHEST
LANES = 128
VMEM_LIMIT = 24 * 1024 * 1024

RIM_X0, RIM_Y0 = 3, 4
RIM_1 = 8
RIM_2 = 6


def roll(value, shift, axis):
    return pltpu.roll(value, shift % value.shape[axis], axis)


def iota(shape, dim):
    return lax.broadcasted_iota(jnp.int32, shape, dim)


def shared_matrix(rows, cols, ratio_rows, ratio_cols, value):
    match = iota((rows, cols), 0) // ratio_rows == iota((rows, cols), 1) // ratio_cols
    return jnp.where(match, value, 0.0).astype(F32)


def dot(left, right):
    return jnp.dot(left, right, precision=HIGHEST, preferred_element_type=F32)


def low_half(shape):
    return iota(shape, 0) < 4


def shifted_tiles(first, second, left, right):
    low = low_half(first.shape)
    a, b = roll(first, 4, 0), roll(second, 4, 0)
    return jnp.where(low, left, a), jnp.where(low, a, b), jnp.where(low, b, right)


def row_mask(shape, first_row, last_row, origin, size, lanes=None):
    row = iota(shape, 0)
    place = row + origin
    good = (row >= first_row) & (row < last_row) & (place >= 0) & (place < size)
    if lanes is not None:
        good = good & (iota(shape, 1) < lanes)
    return jnp.where(good, 1.0, 0.0).astype(F32)


def plane_bar(place, size):
    return jnp.where((place >= 0) & (place < size), 0.5, 2.0).astype(F32)


def over_planes(first, last, step, unroll=1):
    def loop_body(x, carry):
        step(x)
        return carry

    lax.fori_loop(first, last, loop_body, 0, unroll=unroll)


def fill_weights(e_ref, weights, planes, scale, wrap_free):
    wx, wy, wz, wb, total = weights
    half = 0.5 * scale
    shape = e_ref.shape[1:]
    lane = iota(shape, 1)
    last = shape[1] - 1

    def along_x(x):
        wx[x] = half * (e_ref[x] + e_ref[x + 1])

    over_planes(0, planes - 1, along_x)

    def others(x):
        e = e_ref[x]
        y = half * (e + roll(e, -1, 0))
        z = half * (e + roll(e, -1, 1))
        if not wrap_free:
            z = jnp.where(lane < last, z, 0.0)
        faces = (wx[x] + wx[x - 1]) + (y + roll(y, 1, 0)) + (z + roll(z, 1, 1))
        if not wrap_free:
            b = jnp.where((lane == 0) | (lane == last), half * e, 0.0)
            wb[x] = b
            faces = faces + b
        wy[x] = y
        wz[x] = z
        total[x] = faces

    over_planes(1, planes - 1, others)


def flux_of(x, u_ref, weights):
    wx, wy, wz, wb, _ = weights
    u = u_ref[x]
    py = wy[x] * (roll(u, -1, 0) - u)
    pz = wz[x] * (roll(u, -1, 1) - u)
    flux = wx[x - 1] * (u - u_ref[x - 1]) - wx[x] * (u_ref[x + 1] - u)
    flux = flux + (roll(py, 1, 0) - py) + (roll(pz, 1, 1) - pz)
    if wb is not None:
        flux = flux + wb[x] * u
    return u, flux


def halves(u):
    return jnp.exp(u - LN2), jnp.exp(-u - LN2)


def sweep(u_ref, out_ref, weights, k_ref, f_ref, first, last, rows, origin, size):
    def step(x):
        u, flux = flux_of(x, u_ref, weights)
        up, down = halves(u)
        k = k_ref[x]
        defect = f_ref[x] - (flux + k * (up - down))
        slope = weights[4][x] + k * (up + down)
        moved = u + OMEGA * defect / slope
        out_ref[x] = jnp.where(rows > plane_bar(origin + x, size), moved, 0.0)

    over_planes(first, last, step)


def defect_at(x, u_ref, weights, k_ref, load):
    u, flux = flux_of(x, u_ref, weights)
    up, down = halves(u)
    return load - (flux + k_ref[x] * (up - down))


def pair_rows(ref, base, count=8):
    return ref[pl.ds(base, count, 2), :] + ref[pl.ds(base + 1, count, 2), :]


def rim_plane(x, brick, left, right, base, depth, rim):
    size = brick.shape[0]
    if x < rim:
        at = x - (rim - depth)
        return (left, base + at) if at >= 0 else None
    if x < rim + size:
        return (brick, x - rim)
    at = x - rim - size
    return (right, base + at) if at < depth else None


FINE_SENT = ((3, 0), (3, 3), (2, 6), (2, 8))


def fine_plane(x, index, brick, left, right):
    depth, base = FINE_SENT[index]
    return rim_plane(x, brick, left, right, base, depth, RIM_X0)


def tile_of(place, tile):
    if place is None:
        return None
    ref, x = place
    return ref[x, 8 * tile : 8 * tile + 8, :]


def pack_fine(s_ref, e_ref, k_ref, f_ref, xl_ref, xr_ref, up_ref, down_ref):
    bricks = (s_ref, e_ref, k_ref, f_ref)
    planes = s_ref.shape[0] + 2 * RIM_X0
    shape = (8, s_ref.shape[2])
    low = low_half(shape)
    zero = jnp.zeros(shape, F32)
    for x in range(planes):
        for pair in range(2):
            places = [fine_plane(x, 2 * pair + i, bricks[2 * pair + i], xl_ref, xr_ref) for i in range(2)]
            if places[0] is None:
                up_ref[pair, x] = zero
                down_ref[pair, x] = zero
                continue
            up_ref[pair, x] = jnp.where(low, roll(tile_of(places[0], 1), 4, 0), tile_of(places[1], 1))
            down_ref[pair, x] = jnp.where(low, tile_of(places[0], 0), roll(tile_of(places[1], 0), 4, 0))


def fine_first(
    s_ref, e_ref, k_ref, f_ref, xl_ref, xr_ref, yl_ref, yr_ref,
    stack_ref, u0_ref, ew_ref, kw_ref, fw_ref,
    ua, ub, wx, wy, wz, wb, total, gather, summed,
    *, size_x, size_y,
):
    bricks = (s_ref, e_ref, k_ref, f_ref)
    windows = (ua, ew_ref, kw_ref, fw_ref)
    own_x, own_y, nz = s_ref.shape
    planes = own_x + 2 * RIM_X0
    rows = own_y + 2 * RIM_Y0
    for x in range(planes):
        for index in range(4):
            place = fine_plane(x, index, bricks[index], xl_ref, xr_ref)
            if place is None:
                windows[index][x] = jnp.zeros((rows, nz), F32)
                continue
            left, right = yl_ref[index // 2, x], yr_ref[index // 2, x]
            if index % 2 == 0:
                right = roll(right, 4, 0)
            else:
                left = roll(left, 4, 0)
            tiles = shifted_tiles(tile_of(place, 0), tile_of(place, 1), left, right)
            for i, tile in enumerate(tiles):
                windows[index][x, 8 * i : 8 * i + 8, :] = tile
    weights = (wx, wy, wz, wb, total)
    fill_weights(ew_ref, weights, planes, 1.0, False)
    origin_x = lax.axis_index("gx") * own_x - RIM_X0
    origin_y = lax.axis_index("gy") * own_y - RIM_Y0
    shape = (rows, nz)
    mask = row_mask(shape, 2, rows - 2, origin_y, size_y)
    sweep(ua, ub, weights, kw_ref, fw_ref, 1, planes - 1, mask, origin_x, size_x)
    mask = row_mask(shape, 3, rows - 3, origin_y, size_y)
    sweep(ub, ua, weights, kw_ref, fw_ref, 2, planes - 2, mask, origin_x, size_x)

    low = low_half((8, nz))
    pairs = own_x // 2

    def finish(j):
        x = RIM_X0 + 2 * j
        gather[pl.ds(j * rows, rows), :] = ua[x] + ua[x + 1]
        d = defect_at(x, ua, weights, kw_ref, fw_ref[x]) + defect_at(x + 1, ua, weights, kw_ref, fw_ref[x + 1])
        gather[pl.ds((pairs + j) * rows, rows), :] = d
        for i in range(2):
            u = ua[x + i]
            moved = [roll(u[8 * t : 8 * t + 8], 4, 0) for t in range(3)]
            u0_ref[2 * j + i, 0:8, :] = jnp.where(low, moved[0], moved[1])
            u0_ref[2 * j + i, 8:16, :] = jnp.where(low, moved[1], moved[2])

    over_planes(0, pairs, finish)
    base = 2 * pairs * rows
    for i, ref in enumerate((e_ref, k_ref)):
        for j in range(pairs):
            at = base + (i * pairs + j) * own_y
            gather[at : at + own_y, :] = ref[2 * j] + ref[2 * j + 1]
    summed[...] = dot(gather[...], shared_matrix(nz, nz // 2, 2, 1, 0.125))
    for j in range(pairs):
        stack_ref[0, j] = pair_rows(summed, base + j * own_y)
        stack_ref[1, j] = pair_rows(summed, base + (pairs + j) * own_y)
        stack_ref[2, j] = pair_rows(summed, j * rows + RIM_Y0)
        stack_ref[3, j] = pair_rows(summed, (pairs + j) * rows + RIM_Y0)


def middle_first(
    l_ref, o_ref, r_ref, u0_ref,
    up_ref, down_ref, stack_ref, w_ref, f_ref,
    e, k, v, wa, wx, wy, wz, wb, total, gather, summed,
    *, size_x, size_y,
):
    planes, own, nz = o_ref.shape[1:]
    rows = own + 2 * RIM_1
    shape = (rows, nz)

    def joined(index, x):
        return jnp.concatenate([l_ref[index, x], o_ref[index, x], r_ref[index, x]], axis=0)

    def assemble(x):
        e[x] = joined(0, x)
        k[x] = joined(1, x)
        v[x] = joined(2, x)

    over_planes(0, planes, assemble)
    weights = (wx, wy, wz, wb, total)
    fill_weights(e, weights, planes, 0.25, False)
    origin_x = lax.axis_index("gx") * own - RIM_1
    origin_y = lax.axis_index("gy") * own - RIM_1

    def load(x):
        f_ref[x] = defect_at(x, v, weights, k, joined(3, x))

    over_planes(2, planes - 2, load)
    mask = row_mask(shape, 2, rows - 2, origin_y, size_y)
    sweep(v, wa, weights, k, f_ref, 2, planes - 2, mask, origin_x, size_x)
    mask = row_mask(shape, 3, rows - 3, origin_y, size_y)
    sweep(wa, w_ref, weights, k, f_ref, 3, planes - 3, mask, origin_x, size_x)
    pairs = (planes - 8) // 2

    def finish(j):
        x = 4 + 2 * j
        d = defect_at(x, w_ref, weights, k, f_ref[x]) + defect_at(x + 1, w_ref, weights, k, f_ref[x + 1])
        at = pl.ds(j * rows, rows)
        gather[at, :nz] = e[x] + e[x + 1]
        gather[at, nz:] = k[x] + k[x + 1]
        at = pl.ds((pairs + j) * rows, rows)
        gather[at, :nz] = w_ref[x] + w_ref[x + 1]
        gather[at, nz:] = d

    over_planes(0, pairs, finish)
    summed[...] = dot(gather[...], shared_matrix(2 * nz, nz, 2, 1, 0.125))
    own_planes = u0_ref.shape[0]
    for a in range(2):
        for j in range(pairs):
            tile = pair_rows(summed, (a * pairs + j) * rows + 4)
            stack_ref[a, j] = tile
            if j < RIM_2:
                up_ref[a * RIM_2 + j] = tile
            if j >= pairs - RIM_2:
                down_ref[a * RIM_2 + j - (pairs - RIM_2)] = tile
    for x in range(RIM_X0):
        for t in range(4):
            rows_at, lanes_at = 8 * (t // 2), LANES * (t % 2)
            at = 2 * RIM_2 + 4 * x + t
            up_ref[at] = u0_ref[own_planes - RIM_X0 + x, rows_at : rows_at + 8, lanes_at : lanes_at + LANES]
            down_ref[at] = u0_ref[x, rows_at : rows_at + 8, lanes_at : lanes_at + LANES]


def pack_coarse(xl_ref, xr_ref, stack_ref, u0_ref, up_ref, down_ref, own_ref, rim_ref):
    spare = stack_ref.shape[1] // 2 - 2
    planes = 2 * RIM_2 + 4
    low = low_half((8, LANES))
    for a in range(2):
        for x in range(planes):
            if x < RIM_2:
                tile = xl_ref[a * RIM_2 + x]
            elif x < RIM_2 + 4:
                tile = stack_ref[a, x - RIM_2 + spare]
            else:
                tile = xr_ref[a * RIM_2 + x - RIM_2 - 4]
            at = a * planes + x
            own_ref[at] = tile
            up_ref[at] = tile
            down_ref[at] = tile
    own_planes = u0_ref.shape[0]
    base = 2 * RIM_2
    for x in range(own_planes + 2 * RIM_X0):
        if x < RIM_X0:
            tiles = [xl_ref[base + 4 * x + t] for t in range(4)]
        elif x < RIM_X0 + own_planes:
            tiles = [
                u0_ref[x - RIM_X0, 8 * (t // 2) : 8 * (t // 2) + 8, LANES * (t % 2) : LANES * (t % 2) + LANES]
                for t in range(4)
            ]
        else:
            tiles = [xr_ref[base + 4 * (x - RIM_X0 - own_planes) + t] for t in range(4)]
        at = 2 * planes + x
        up_ref[at] = jnp.where(low, roll(tiles[2], 4, 0), tiles[3])
        down_ref[at] = jnp.where(low, tiles[0], roll(tiles[1], 4, 0))
        for t in range(4):
            rim_ref[x, 8 * (t // 2) : 8 * (t // 2) + 8, LANES * (t % 2) : LANES * (t % 2) + LANES] = tiles[t]


def coarse_and_last(
    l1_ref, o1_ref, r1_ref, w1_ref, f1_ref, yl_ref, yr_ref, o2_ref, u0_ref, ew_ref, kw_ref, fw_ref,
    out_ref, part_ref,
    e2, k2, v2, f2, a2, b2, wx2, wy2, wz2, t2, q2, s2, d2,
    e1, k1, a1, b1, wx1, wy1, wz1, wb1, t1, d1,
    a0, b0, wx0, wy0, wz0, wb0, t0, q0,
    *, size_x, size_y,
):
    place_x, place_y = lax.axis_index("gx"), lax.axis_index("gy")
    planes2 = 2 * RIM_2 + 4
    rows2 = planes2
    shape2 = (rows2, LANES)
    nz2 = LANES // 2
    row8 = iota((8, LANES), 0)
    inside = iota(shape2, 1) < nz2

    def window2(at):
        own = roll(o2_ref[at], 4, 0)
        upper = jnp.where(row8 >= 6, own, yl_ref[at])
        lower = jnp.where(row8 < 2, own, yr_ref[at])
        return jnp.concatenate([upper, lower], axis=0)

    def assemble2(x):
        both = window2(x)
        e2[x] = jnp.where(inside, both, 0.0)
        k2[x] = jnp.where(inside, roll(both, nz2, 1), 0.0)
        both = window2(planes2 + x)
        v2[x] = jnp.where(inside, both, 0.0)
        f2[x] = jnp.where(inside, roll(both, nz2, 1), 0.0)

    over_planes(0, planes2, assemble2)
    weights2 = (wx2, wy2, wz2, None, t2)
    fill_weights(e2, weights2, planes2, 0.0625, True)
    origin_x = place_x * 4 - RIM_2
    origin_y = place_y * 4 - RIM_2

    def load2(x):
        f2[x] = defect_at(x, v2, weights2, k2, f2[x])

    over_planes(1, planes2 - 1, load2)
    source = v2
    for i in range(4):
        target = a2 if i % 2 == 0 else b2
        mask = row_mask(shape2, 1 + i, rows2 - 1 - i, origin_y, size_y // 4, nz2)
        sweep(source, target, weights2, k2, f2, 1 + i, planes2 - 1 - i, mask, origin_x, size_x // 4)
        source = target
    for j in range(8):
        q2[16 * j : 16 * j + 16, :] = source[4 + j] - v2[4 + j]
    s2[...] = dot(q2[...], shared_matrix(LANES, LANES, 1, 2, 1.0))
    rows1 = o1_ref.shape[2] + 2 * RIM_1
    d2[...] = jnp.zeros(d2.shape, F32)
    for j in range(8):
        rows = roll(s2[16 * j : 16 * j + 16, :], -4, 0)[:8]
        d2[pl.ds(rows1 * j + 4, 8, 2), :] = rows
        d2[pl.ds(rows1 * j + 5, 8, 2), :] = rows

    planes1, own1, nz1 = o1_ref.shape[1:]
    shape1 = (rows1, nz1)

    def joined(index, x):
        return jnp.concatenate([l1_ref[index, x], o1_ref[index, x], r1_ref[index, x]], axis=0)

    def assemble1(x):
        e1[x] = joined(0, x)
        k1[x] = joined(1, x)

    over_planes(0, planes1, assemble1)
    weights1 = (wx1, wy1, wz1, wb1, t1)
    fill_weights(e1, weights1, planes1, 0.25, False)
    origin_x = place_x * own1 - RIM_1
    origin_y = place_y * own1 - RIM_1
    for x in range(4, 20):
        at = rows1 * ((x - 4) // 2)
        a1[x] = w1_ref[x] + d2[at : at + rows1, :]
    mask = row_mask(shape1, 5, rows1 - 5, origin_y, size_y // 2)
    sweep(a1, b1, weights1, k1, f1_ref, 5, planes1 - 5, mask, origin_x, size_x // 2)
    mask = row_mask(shape1, 6, rows1 - 6, origin_y, size_y // 2)
    sweep(b1, a1, weights1, k1, f1_ref, 6, planes1 - 6, mask, origin_x, size_x // 2)
    for j in range(12):
        rows = roll(a1[6 + j] - joined(2, 6 + j), -6, 0)[:16]
        d1[pl.ds(32 * j, 16, 2), :] = rows
        d1[pl.ds(32 * j + 1, 16, 2), :] = rows
    nz0 = 2 * nz1
    q0[...] = dot(d1[...], shared_matrix(nz1, nz0, 1, 2, 1.0))

    own_x, own_y = out_ref.shape[:2]
    planes0 = own_x + 2 * RIM_X0
    rows0 = own_y + 2 * RIM_Y0
    shape0 = (rows0, nz0)
    base = 2 * planes2
    for x in range(planes0):
        left, right = yl_ref[base + x], yr_ref[base + x]
        left = jnp.concatenate([left, roll(left, 4, 0)], axis=1)
        right = jnp.concatenate([roll(right, 4, 0), right], axis=1)
        tiles = shifted_tiles(u0_ref[x, 0:8, :], u0_ref[x, 8:16, :], left, right)
        at = 32 * ((x + 1) // 2)
        for i, tile in enumerate(tiles):
            a0[x, 8 * i : 8 * i + 8, :] = tile + q0[at + 8 * i : at + 8 * i + 8, :]
    weights0 = (wx0, wy0, wz0, wb0, t0)
    fill_weights(ew_ref, weights0, planes0, 1.0, False)
    origin_x = place_x * own_x - RIM_X0
    origin_y = place_y * own_y - RIM_Y0
    mask = row_mask(shape0, 2, rows0 - 2, origin_y, size_y)
    sweep(a0, b0, weights0, kw_ref, fw_ref, 1, planes0 - 1, mask, origin_x, size_x)
    mask = row_mask(shape0, 3, rows0 - 3, origin_y, size_y)
    sweep(b0, a0, weights0, kw_ref, fw_ref, 2, planes0 - 2, mask, origin_x, size_x)
    low = low_half((8, nz0))

    def finish(x, acc):
        d = defect_at(x, a0, weights0, kw_ref, fw_ref[x])
        u = a0[x]
        moved = [roll(u[8 * t : 8 * t + 8], 4, 0) for t in range(3)]
        out_ref[x - RIM_X0, 0:8, :] = jnp.where(low, moved[0], moved[1])
        out_ref[x - RIM_X0, 8:16, :] = jnp.where(low, moved[1], moved[2])
        return acc + d * d

    acc = lax.fori_loop(RIM_X0, RIM_X0 + own_x, finish, jnp.zeros(shape0, F32))
    row = iota(shape0, 0)
    acc = jnp.where((row >= RIM_Y0) & (row < RIM_Y0 + own_y), acc, 0.0)
    acc = jnp.sum(acc, axis=0, keepdims=True)
    acc = acc[:, :LANES] + acc[:, LANES:]
    part_ref[...] = jnp.broadcast_to(acc, part_ref.shape)


def arr(*shape):
    return jax.ShapeDtypeStruct(shape, F32)


def call(kernel, outs, scratch, *args):
    return pl.pallas_call(
        kernel,
        out_shape=outs,
        in_specs=[pl.BlockSpec(memory_space=pltpu.VMEM)] * len(args),
        out_specs=[pl.BlockSpec(memory_space=pltpu.VMEM)] * len(outs),
        scratch_shapes=[pltpu.VMEM(shape, F32) for shape in scratch],
        compiler_params=pltpu.CompilerParams(vmem_limit_bytes=VMEM_LIMIT),
    )(*args)


def swap(upward, downward, axis):
    size = lax.axis_size(axis)
    up = [(i, i + 1) for i in range(size - 1)]
    down = [(j, i) for i, j in up]
    return lax.ppermute(upward, axis, up), lax.ppermute(downward, axis, down)


def sum_over(part, axis):
    size = lax.axis_size(axis)
    rows = jnp.broadcast_to(part, (size, LANES))
    return jnp.sum(lax.all_to_all(rows, axis, 0, 0, tiled=True), axis=0, keepdims=True)


def body(start, permit, ion, source):
    own_x, own_y, nz = start.shape
    size_x, size_y = own_x * lax.axis_size("gx"), own_y * lax.axis_size("gy")
    planes0, rows0 = own_x + 2 * RIM_X0, own_y + 2 * RIM_Y0
    window0 = (planes0, rows0, nz)

    fields = (start, permit, ion, source)
    depths = [depth for depth, _ in FINE_SENT]
    upward = jnp.concatenate([a[own_x - d :] for a, d in zip(fields, depths)], axis=0)
    downward = jnp.concatenate([a[:d] for a, d in zip(fields, depths)], axis=0)
    xl, xr = swap(upward, downward, "gx")
    packed = arr(2, planes0, 8, nz)
    upward, downward = call(pack_fine, [packed, packed], [], *fields, xl, xr)
    yl, yr = swap(upward, downward, "gy")
    own1, own1_y, nz1 = own_x // 2, own_y // 2, nz // 2
    gathered = 2 * own1 * rows0 + 2 * own1 * own_y
    stack1, u0, permit0, ion0, source0 = call(
        functools.partial(fine_first, size_x=size_x, size_y=size_y),
        [arr(4, own1, own1_y, nz1), arr(own_x, own_y, nz)] + [arr(*window0)] * 3,
        [window0] * 7 + [(gathered, nz), (gathered, nz1)],
        *fields, xl, xr, yl, yr,
    )

    xl, xr = swap(stack1, stack1, "gx")
    own = jnp.concatenate([xl, stack1, xr], axis=1)
    yl1, yr1 = swap(own, own, "gy")
    planes1 = own1 + 2 * RIM_1
    window1 = (planes1, own1_y + 2 * RIM_1, nz1)
    sent_x = 2 * RIM_2 + 4 * RIM_X0
    upward, downward, stack2, w1, f1 = call(
        functools.partial(middle_first, size_x=size_x // 2, size_y=size_y // 2),
        [arr(sent_x, 8, LANES)] * 2 + [arr(2, 8, 8, LANES)] + [arr(*window1)] * 2,
        [window1] * 9 + [(16 * window1[1], 2 * nz1), (16 * window1[1], nz1)],
        yl1, own, yr1, u0,
    )

    xl, xr = swap(upward, downward, "gx")
    planes2 = 2 * RIM_2 + 4
    sent_y = 2 * planes2 + planes0
    upward, downward, own2, rim0 = call(
        pack_coarse,
        [arr(sent_y, 8, LANES)] * 2 + [arr(2 * planes2, 8, LANES), arr(planes0, own_y, nz)],
        [], xl, xr, stack2, u0,
    )
    yl, yr = swap(upward, downward, "gy")
    window2 = (planes2, planes2, LANES)
    relaxed, part = call(
        functools.partial(coarse_and_last, size_x=size_x, size_y=size_y),
        [arr(own_x, own_y, nz), arr(8, LANES)],
        [window2] * 10 + [(LANES, LANES)] * 2 + [(8 * window1[1], LANES)]
        + [window1] * 9 + [(12 * 32, nz1)] + [window0] * 7 + [(12 * 32, nz)],
        yl1, own, yr1, w1, f1, yl, yr, own2, rim0, permit0, ion0, source0,
    )
    total = jnp.sum(sum_over(sum_over(part[:1], "gx"), "gy"))
    return relaxed, jnp.sqrt(total / (size_x * size_y * nz))


def solution(mesh):
    specs = (P("gx", "gy", None),) * 4
    return jax.shard_map(
        body, mesh=mesh, in_specs=specs, out_specs=(P("gx", "gy", None), P()), check_vma=False
    )
```

```python
import functools

import jax
import jax.numpy as jnp
from jax import lax
from jax.experimental import pallas as pl
from jax.experimental.pallas import tpu as pltpu
from jax.sharding import PartitionSpec as P

OMEGA = 0.8
LN2 = 0.6931471805599453
F32 = jnp.float32
HIGHEST = lax.Precision.HIGHEST
LANES = 128
VMEM_LIMIT = 24 * 1024 * 1024

RIM_X0, RIM_Y0 = 3, 4
RIM_1 = 8
RIM_2 = 6


def roll(value, shift, axis):
    return pltpu.roll(value, shift % value.shape[axis], axis)


def iota(shape, dim):
    return lax.broadcasted_iota(jnp.int32, shape, dim)


def shared_matrix(rows, cols, ratio_rows, ratio_cols, value):
    match = iota((rows, cols), 0) // ratio_rows == iota((rows, cols), 1) // ratio_cols
    return jnp.where(match, value, 0.0).astype(F32)


def dot(left, right):
    return jnp.dot(left, right, precision=HIGHEST, preferred_element_type=F32)


def low_half(shape):
    return iota(shape, 0) < 4


def shifted_tiles(first, second, left, right):
    low = low_half(first.shape)
    a, b = roll(first, 4, 0), roll(second, 4, 0)
    return jnp.where(low, left, a), jnp.where(low, a, b), jnp.where(low, b, right)


def row_mask(shape, first_row, last_row, origin, size, lanes=None):
    row = iota(shape, 0)
    place = row + origin
    good = (row >= first_row) & (row < last_row) & (place >= 0) & (place < size)
    if lanes is not None:
        good = good & (iota(shape, 1) < lanes)
    return jnp.where(good, 1.0, 0.0).astype(F32)


def inner_sides(shape):
    place, last = lax.axis_index("gy"), lax.axis_size("gy") - 1
    row = iota(shape, 0)
    return row >= jnp.where(place == 0, shape[0], 0), row >= jnp.where(place == last, shape[0], 0)


def plane_bar(place, size):
    return jnp.where((place >= 0) & (place < size), 0.5, 2.0).astype(F32)


def over_planes(first, last, step):
    def loop_body(x, carry):
        step(x)
        return carry

    lax.fori_loop(first, last, loop_body, 0, unroll=last - first)


def fill_weights(e_ref, weights, planes, scale, wrap_free):
    wx, wy, wz, wb, total = weights
    half = 0.5 * scale
    shape = e_ref.shape[1:]
    lane = iota(shape, 1)
    last = shape[1] - 1

    def along_x(x):
        wx[x] = half * (e_ref[x] + e_ref[x + 1])

    over_planes(0, planes - 1, along_x)

    def others(x):
        e = e_ref[x]
        y = half * (e + roll(e, -1, 0))
        z = half * (e + roll(e, -1, 1))
        if not wrap_free:
            z = jnp.where(lane < last, z, 0.0)
        faces = (wx[x] + wx[x - 1]) + (y + roll(y, 1, 0)) + (z + roll(z, 1, 1))
        if not wrap_free:
            b = jnp.where((lane == 0) | (lane == last), half * e, 0.0)
            wb[x] = b
            faces = faces + b
        wy[x] = y
        wz[x] = z
        total[x] = faces

    over_planes(1, planes - 1, others)


def flux_of(x, u_ref, weights):
    wx, wy, wz, wb, _ = weights
    u = u_ref[x]
    py = wy[x] * (roll(u, -1, 0) - u)
    pz = wz[x] * (roll(u, -1, 1) - u)
    flux = wx[x - 1] * (u - u_ref[x - 1]) - wx[x] * (u_ref[x + 1] - u)
    flux = flux + (roll(py, 1, 0) - py) + (roll(pz, 1, 1) - pz)
    if wb is not None:
        flux = flux + wb[x] * u
    return u, flux


def halves(u):
    return jnp.exp(u - LN2), jnp.exp(-u - LN2)


def sweep(u_ref, out_ref, weights, k_ref, f_ref, first, last, rows, origin, size):
    def step(x):
        u, flux = flux_of(x, u_ref, weights)
        up, down = halves(u)
        k = k_ref[x]
        defect = f_ref[x] - (flux + k * (up - down))
        slope = weights[4][x] + k * (up + down)
        moved = u + OMEGA * defect / slope
        out_ref[x] = jnp.where(rows > plane_bar(origin + x, size), moved, 0.0)

    over_planes(first, last, step)


def defect_at(x, u_ref, weights, k_ref, load):
    u, flux = flux_of(x, u_ref, weights)
    up, down = halves(u)
    return load - (flux + k_ref[x] * (up - down))


def pair_rows(ref, base, count=8):
    return ref[pl.ds(base, count, 2), :] + ref[pl.ds(base + 1, count, 2), :]


def rim_plane(x, brick, left, right, base, depth, rim):
    size = brick.shape[0]
    if x < rim:
        at = x - (rim - depth)
        return (left, base + at) if at >= 0 else None
    if x < rim + size:
        return (brick, x - rim)
    at = x - rim - size
    return (right, base + at) if at < depth else None


FINE_SENT = ((3, 0), (3, 3), (2, 6), (2, 8))


def fine_plane(x, index, brick, left, right):
    depth, base = FINE_SENT[index]
    return rim_plane(x, brick, left, right, base, depth, RIM_X0)


def tile_of(place, tile):
    if place is None:
        return None
    ref, x = place
    return ref[x, 8 * tile : 8 * tile + 8, :]


def pack_fine(s_ref, e_ref, k_ref, f_ref, xl_ref, xr_ref, up_ref, down_ref):
    bricks = (s_ref, e_ref, k_ref, f_ref)
    planes = s_ref.shape[0] + 2 * RIM_X0
    shape = (8, s_ref.shape[2])
    low = low_half(shape)
    zero = jnp.zeros(shape, F32)
    for x in range(planes):
        for pair in range(2):
            places = [fine_plane(x, 2 * pair + i, bricks[2 * pair + i], xl_ref, xr_ref) for i in range(2)]
            if places[0] is None:
                up_ref[pair, x] = zero
                down_ref[pair, x] = zero
                continue
            up_ref[pair, x] = jnp.where(low, roll(tile_of(places[0], 1), 4, 0), tile_of(places[1], 1))
            down_ref[pair, x] = jnp.where(low, tile_of(places[0], 0), roll(tile_of(places[1], 0), 4, 0))


def fine_first(
    s_ref, e_ref, k_ref, f_ref, xl_ref, xr_ref, yl_ref, yr_ref,
    stack_ref, u0_ref, ew_ref, kw_ref, fw_ref,
    ua, ub, wx, wy, wz, wb, total, gather, summed,
    *, size_x, size_y,
):
    bricks = (s_ref, e_ref, k_ref, f_ref)
    windows = (ua, ew_ref, kw_ref, fw_ref)
    own_x, own_y, nz = s_ref.shape
    planes = own_x + 2 * RIM_X0
    rows = own_y + 2 * RIM_Y0
    keep_left, keep_right = inner_sides((8, nz))
    for x in range(planes):
        for index in range(4):
            place = fine_plane(x, index, bricks[index], xl_ref, xr_ref)
            if place is None:
                windows[index][x] = jnp.zeros((rows, nz), F32)
                continue
            left = jnp.where(keep_left, yl_ref[index // 2, x], 0.0)
            right = jnp.where(keep_right, yr_ref[index // 2, x], 0.0)
            if index % 2 == 0:
                right = roll(right, 4, 0)
            else:
                left = roll(left, 4, 0)
            tiles = shifted_tiles(tile_of(place, 0), tile_of(place, 1), left, right)
            for i, tile in enumerate(tiles):
                windows[index][x, 8 * i : 8 * i + 8, :] = tile
    weights = (wx, wy, wz, wb, total)
    fill_weights(ew_ref, weights, planes, 1.0, False)
    origin_x = lax.axis_index("gx") * own_x - RIM_X0
    origin_y = lax.axis_index("gy") * own_y - RIM_Y0
    shape = (rows, nz)
    mask = row_mask(shape, 2, rows - 2, origin_y, size_y)
    sweep(ua, ub, weights, kw_ref, fw_ref, 1, planes - 1, mask, origin_x, size_x)
    mask = row_mask(shape, 3, rows - 3, origin_y, size_y)
    sweep(ub, ua, weights, kw_ref, fw_ref, 2, planes - 2, mask, origin_x, size_x)

    low = low_half((8, nz))
    pairs = own_x // 2

    def finish(j):
        x = RIM_X0 + 2 * j
        gather[pl.ds(j * rows, rows), :] = ua[x] + ua[x + 1]
        d = defect_at(x, ua, weights, kw_ref, fw_ref[x]) + defect_at(x + 1, ua, weights, kw_ref, fw_ref[x + 1])
        gather[pl.ds((pairs + j) * rows, rows), :] = d
        for i in range(2):
            u = ua[x + i]
            moved = [roll(u[8 * t : 8 * t + 8], 4, 0) for t in range(3)]
            u0_ref[2 * j + i, 0:8, :] = jnp.where(low, moved[0], moved[1])
            u0_ref[2 * j + i, 8:16, :] = jnp.where(low, moved[1], moved[2])

    over_planes(0, pairs, finish)
    base = 2 * pairs * rows
    for i, ref in enumerate((e_ref, k_ref)):
        for j in range(pairs):
            at = base + (i * pairs + j) * own_y
            gather[at : at + own_y, :] = ref[2 * j] + ref[2 * j + 1]
    summed[...] = dot(gather[...], shared_matrix(nz, nz // 2, 2, 1, 0.125))
    for j in range(pairs):
        stack_ref[0, j] = pair_rows(summed, base + j * own_y)
        stack_ref[1, j] = pair_rows(summed, base + (pairs + j) * own_y)
        stack_ref[2, j] = pair_rows(summed, j * rows + RIM_Y0)
        stack_ref[3, j] = pair_rows(summed, (pairs + j) * rows + RIM_Y0)


def middle_first(
    l_ref, o_ref, r_ref, u0_ref,
    up_ref, down_ref, stack_ref, w_ref, f_ref,
    e, k, v, wa, wx, wy, wz, wb, total, gather, summed,
    *, size_x, size_y,
):
    planes, own, nz = o_ref.shape[1:]
    rows = own + 2 * RIM_1
    shape = (rows, nz)
    keep_left, keep_right = inner_sides((own, nz))

    def joined(index, x):
        left = jnp.where(keep_left, l_ref[index, x], 0.0)
        right = jnp.where(keep_right, r_ref[index, x], 0.0)
        return jnp.concatenate([left, o_ref[index, x], right], axis=0)

    def assemble(x):
        e[x] = joined(0, x)
        k[x] = joined(1, x)
        v[x] = joined(2, x)

    over_planes(0, planes, assemble)
    weights = (wx, wy, wz, wb, total)
    fill_weights(e, weights, planes, 0.25, False)
    origin_x = lax.axis_index("gx") * own - RIM_1
    origin_y = lax.axis_index("gy") * own - RIM_1

    def load(x):
        f_ref[x] = defect_at(x, v, weights, k, joined(3, x))

    over_planes(2, planes - 2, load)
    mask = row_mask(shape, 2, rows - 2, origin_y, size_y)
    sweep(v, wa, weights, k, f_ref, 2, planes - 2, mask, origin_x, size_x)
    mask = row_mask(shape, 3, rows - 3, origin_y, size_y)
    sweep(wa, w_ref, weights, k, f_ref, 3, planes - 3, mask, origin_x, size_x)
    pairs = (planes - 8) // 2

    def finish(j):
        x = 4 + 2 * j
        d = defect_at(x, w_ref, weights, k, f_ref[x]) + defect_at(x + 1, w_ref, weights, k, f_ref[x + 1])
        at = pl.ds(j * rows, rows)
        gather[at, :nz] = e[x] + e[x + 1]
        gather[at, nz:] = k[x] + k[x + 1]
        at = pl.ds((pairs + j) * rows, rows)
        gather[at, :nz] = w_ref[x] + w_ref[x + 1]
        gather[at, nz:] = d

    over_planes(0, pairs, finish)
    summed[...] = dot(gather[...], shared_matrix(2 * nz, nz, 2, 1, 0.125))
    own_planes = u0_ref.shape[0]
    for a in range(2):
        for j in range(pairs):
            tile = pair_rows(summed, (a * pairs + j) * rows + 4)
            stack_ref[a, j] = tile
            if j < RIM_2:
                up_ref[a * RIM_2 + j] = tile
            if j >= pairs - RIM_2:
                down_ref[a * RIM_2 + j - (pairs - RIM_2)] = tile
    for x in range(RIM_X0):
        for t in range(4):
            rows_at, lanes_at = 8 * (t // 2), LANES * (t % 2)
            at = 2 * RIM_2 + 4 * x + t
            up_ref[at] = u0_ref[own_planes - RIM_X0 + x, rows_at : rows_at + 8, lanes_at : lanes_at + LANES]
            down_ref[at] = u0_ref[x, rows_at : rows_at + 8, lanes_at : lanes_at + LANES]


def pack_coarse(xl_ref, xr_ref, stack_ref, u0_ref, up_ref, down_ref, own_ref, rim_ref):
    spare = stack_ref.shape[1] // 2 - 2
    planes = 2 * RIM_2 + 4
    low = low_half((8, LANES))
    for a in range(2):
        for x in range(planes):
            if x < RIM_2:
                tile = xl_ref[a * RIM_2 + x]
            elif x < RIM_2 + 4:
                tile = stack_ref[a, x - RIM_2 + spare]
            else:
                tile = xr_ref[a * RIM_2 + x - RIM_2 - 4]
            at = a * planes + x
            own_ref[at] = tile
            up_ref[at] = tile
            down_ref[at] = tile
    own_planes = u0_ref.shape[0]
    base = 2 * RIM_2
    for x in range(own_planes + 2 * RIM_X0):
        if x < RIM_X0:
            tiles = [xl_ref[base + 4 * x + t] for t in range(4)]
        elif x < RIM_X0 + own_planes:
            tiles = [
                u0_ref[x - RIM_X0, 8 * (t // 2) : 8 * (t // 2) + 8, LANES * (t % 2) : LANES * (t % 2) + LANES]
                for t in range(4)
            ]
        else:
            tiles = [xr_ref[base + 4 * (x - RIM_X0 - own_planes) + t] for t in range(4)]
        at = 2 * planes + x
        up_ref[at] = jnp.where(low, roll(tiles[2], 4, 0), tiles[3])
        down_ref[at] = jnp.where(low, tiles[0], roll(tiles[1], 4, 0))
        for t in range(4):
            rim_ref[x, 8 * (t // 2) : 8 * (t // 2) + 8, LANES * (t % 2) : LANES * (t % 2) + LANES] = tiles[t]


def coarse_and_last(
    l1_ref, o1_ref, r1_ref, w1_ref, f1_ref, yl_ref, yr_ref, o2_ref, u0_ref, ew_ref, kw_ref, fw_ref,
    out_ref, part_ref,
    e2, k2, v2, f2, a2, b2, wx2, wy2, wz2, t2, q2, s2, d2,
    e1, k1, a1, b1, wx1, wy1, wz1, wb1, t1, d1,
    a0, b0, wx0, wy0, wz0, wb0, t0, q0,
    *, size_x, size_y,
):
    place_x, place_y = lax.axis_index("gx"), lax.axis_index("gy")
    planes2 = 2 * RIM_2 + 4
    rows2 = planes2
    shape2 = (rows2, LANES)
    nz2 = LANES // 2
    row8 = iota((8, LANES), 0)
    inside = iota(shape2, 1) < nz2
    keep_left, keep_right = inner_sides((8, LANES))

    def window2(at):
        own = roll(o2_ref[at], 4, 0)
        upper = jnp.where(row8 >= 6, own, jnp.where(keep_left, yl_ref[at], 0.0))
        lower = jnp.where(row8 < 2, own, jnp.where(keep_right, yr_ref[at], 0.0))
        return jnp.concatenate([upper, lower], axis=0)

    def assemble2(x):
        both = window2(x)
        e2[x] = jnp.where(inside, both, 0.0)
        k2[x] = jnp.where(inside, roll(both, nz2, 1), 0.0)
        both = window2(planes2 + x)
        v2[x] = jnp.where(inside, both, 0.0)
        f2[x] = jnp.where(inside, roll(both, nz2, 1), 0.0)

    over_planes(0, planes2, assemble2)
    weights2 = (wx2, wy2, wz2, None, t2)
    fill_weights(e2, weights2, planes2, 0.0625, True)
    origin_x = place_x * 4 - RIM_2
    origin_y = place_y * 4 - RIM_2

    def load2(x):
        f2[x] = defect_at(x, v2, weights2, k2, f2[x])

    over_planes(1, planes2 - 1, load2)
    source = v2
    for i in range(4):
        target = a2 if i % 2 == 0 else b2
        mask = row_mask(shape2, 1 + i, rows2 - 1 - i, origin_y, size_y // 4, nz2)
        sweep(source, target, weights2, k2, f2, 1 + i, planes2 - 1 - i, mask, origin_x, size_x // 4)
        source = target
    for j in range(8):
        q2[16 * j : 16 * j + 16, :] = source[4 + j] - v2[4 + j]
    s2[...] = dot(q2[...], shared_matrix(LANES, LANES, 1, 2, 1.0))
    rows1 = o1_ref.shape[2] + 2 * RIM_1
    d2[...] = jnp.zeros(d2.shape, F32)
    for j in range(8):
        rows = roll(s2[16 * j : 16 * j + 16, :], -4, 0)[:8]
        d2[pl.ds(rows1 * j + 4, 8, 2), :] = rows
        d2[pl.ds(rows1 * j + 5, 8, 2), :] = rows

    planes1, own1, nz1 = o1_ref.shape[1:]
    shape1 = (rows1, nz1)

    def joined(index, x):
        left = jnp.where(keep_left, l1_ref[index, x], 0.0)
        right = jnp.where(keep_right, r1_ref[index, x], 0.0)
        return jnp.concatenate([left, o1_ref[index, x], right], axis=0)

    def assemble1(x):
        e1[x] = joined(0, x)
        k1[x] = joined(1, x)

    over_planes(0, planes1, assemble1)
    weights1 = (wx1, wy1, wz1, wb1, t1)
    fill_weights(e1, weights1, planes1, 0.25, False)
    origin_x = place_x * own1 - RIM_1
    origin_y = place_y * own1 - RIM_1
    for x in range(4, 20):
        at = rows1 * ((x - 4) // 2)
        a1[x] = w1_ref[x] + d2[at : at + rows1, :]
    mask = row_mask(shape1, 5, rows1 - 5, origin_y, size_y // 2)
    sweep(a1, b1, weights1, k1, f1_ref, 5, planes1 - 5, mask, origin_x, size_x // 2)
    mask = row_mask(shape1, 6, rows1 - 6, origin_y, size_y // 2)
    sweep(b1, a1, weights1, k1, f1_ref, 6, planes1 - 6, mask, origin_x, size_x // 2)
    for j in range(12):
        rows = roll(a1[6 + j] - joined(2, 6 + j), -6, 0)[:16]
        d1[pl.ds(32 * j, 16, 2), :] = rows
        d1[pl.ds(32 * j + 1, 16, 2), :] = rows
    nz0 = 2 * nz1
    q0[...] = dot(d1[...], shared_matrix(nz1, nz0, 1, 2, 1.0))

    own_x, own_y = out_ref.shape[:2]
    planes0 = own_x + 2 * RIM_X0
    rows0 = own_y + 2 * RIM_Y0
    shape0 = (rows0, nz0)
    base = 2 * planes2
    for x in range(planes0):
        left = jnp.where(keep_left, yl_ref[base + x], 0.0)
        right = jnp.where(keep_right, yr_ref[base + x], 0.0)
        left = jnp.concatenate([left, roll(left, 4, 0)], axis=1)
        right = jnp.concatenate([roll(right, 4, 0), right], axis=1)
        tiles = shifted_tiles(u0_ref[x, 0:8, :], u0_ref[x, 8:16, :], left, right)
        at = 32 * ((x + 1) // 2)
        for i, tile in enumerate(tiles):
            a0[x, 8 * i : 8 * i + 8, :] = tile + q0[at + 8 * i : at + 8 * i + 8, :]
    weights0 = (wx0, wy0, wz0, wb0, t0)
    fill_weights(ew_ref, weights0, planes0, 1.0, False)
    origin_x = place_x * own_x - RIM_X0
    origin_y = place_y * own_y - RIM_Y0
    mask = row_mask(shape0, 2, rows0 - 2, origin_y, size_y)
    sweep(a0, b0, weights0, kw_ref, fw_ref, 1, planes0 - 1, mask, origin_x, size_x)
    mask = row_mask(shape0, 3, rows0 - 3, origin_y, size_y)
    sweep(b0, a0, weights0, kw_ref, fw_ref, 2, planes0 - 2, mask, origin_x, size_x)
    low = low_half((8, nz0))

    def finish(x, acc):
        d = defect_at(x, a0, weights0, kw_ref, fw_ref[x])
        u = a0[x]
        moved = [roll(u[8 * t : 8 * t + 8], 4, 0) for t in range(3)]
        out_ref[x - RIM_X0, 0:8, :] = jnp.where(low, moved[0], moved[1])
        out_ref[x - RIM_X0, 8:16, :] = jnp.where(low, moved[1], moved[2])
        return acc + d * d

    acc = lax.fori_loop(RIM_X0, RIM_X0 + own_x, finish, jnp.zeros(shape0, F32), unroll=own_x)
    row = iota(shape0, 0)
    acc = jnp.where((row >= RIM_Y0) & (row < RIM_Y0 + own_y), acc, 0.0)
    acc = jnp.sum(acc, axis=0, keepdims=True)
    acc = acc[:, :LANES] + acc[:, LANES:]
    part_ref[...] = jnp.broadcast_to(acc, part_ref.shape)


def arr(*shape):
    return jax.ShapeDtypeStruct(shape, F32)


def call(kernel, outs, scratch, *args):
    return pl.pallas_call(
        kernel,
        out_shape=outs,
        in_specs=[pl.BlockSpec(memory_space=pltpu.VMEM)] * len(args),
        out_specs=[pl.BlockSpec(memory_space=pltpu.VMEM)] * len(outs),
        scratch_shapes=[pltpu.VMEM(shape, F32) for shape in scratch],
        compiler_params=pltpu.CompilerParams(vmem_limit_bytes=VMEM_LIMIT),
    )(*args)


def swap(upward, downward, axis, ring=False):
    size = lax.axis_size(axis)
    up = [(i, (i + 1) % size) for i in range(size if ring else size - 1)]
    down = [(j, i) for i, j in up]
    return lax.ppermute(upward, axis, up), lax.ppermute(downward, axis, down)


def sum_over(part, axis):
    size = lax.axis_size(axis)
    rows = jnp.broadcast_to(part, (size, LANES))
    return jnp.sum(lax.all_to_all(rows, axis, 0, 0, tiled=True), axis=0, keepdims=True)


def body(start, permit, ion, source):
    own_x, own_y, nz = start.shape
    size_x, size_y = own_x * lax.axis_size("gx"), own_y * lax.axis_size("gy")
    planes0, rows0 = own_x + 2 * RIM_X0, own_y + 2 * RIM_Y0
    window0 = (planes0, rows0, nz)

    fields = (start, permit, ion, source)
    depths = [depth for depth, _ in FINE_SENT]
    upward = jnp.concatenate([a[own_x - d :] for a, d in zip(fields, depths)], axis=0)
    downward = jnp.concatenate([a[:d] for a, d in zip(fields, depths)], axis=0)
    xl, xr = swap(upward, downward, "gx")
    packed = arr(2, planes0, 8, nz)
    upward, downward = call(pack_fine, [packed, packed], [], *fields, xl, xr)
    yl, yr = swap(upward, downward, "gy", True)
    own1, own1_y, nz1 = own_x // 2, own_y // 2, nz // 2
    gathered = 2 * own1 * rows0 + 2 * own1 * own_y
    stack1, u0, permit0, ion0, source0 = call(
        functools.partial(fine_first, size_x=size_x, size_y=size_y),
        [arr(4, own1, own1_y, nz1), arr(own_x, own_y, nz)] + [arr(*window0)] * 3,
        [window0] * 7 + [(gathered, nz), (gathered, nz1)],
        *fields, xl, xr, yl, yr,
    )

    xl, xr = swap(stack1, stack1, "gx")
    own = jnp.concatenate([xl, stack1, xr], axis=1)
    yl1, yr1 = swap(own, own, "gy", True)
    planes1 = own1 + 2 * RIM_1
    window1 = (planes1, own1_y + 2 * RIM_1, nz1)
    sent_x = 2 * RIM_2 + 4 * RIM_X0
    upward, downward, stack2, w1, f1 = call(
        functools.partial(middle_first, size_x=size_x // 2, size_y=size_y // 2),
        [arr(sent_x, 8, LANES)] * 2 + [arr(2, 8, 8, LANES)] + [arr(*window1)] * 2,
        [window1] * 9 + [(16 * window1[1], 2 * nz1), (16 * window1[1], nz1)],
        yl1, own, yr1, u0,
    )

    xl, xr = swap(upward, downward, "gx")
    planes2 = 2 * RIM_2 + 4
    sent_y = 2 * planes2 + planes0
    upward, downward, own2, rim0 = call(
        pack_coarse,
        [arr(sent_y, 8, LANES)] * 2 + [arr(2 * planes2, 8, LANES), arr(planes0, own_y, nz)],
        [], xl, xr, stack2, u0,
    )
    yl, yr = swap(upward, downward, "gy", True)
    window2 = (planes2, planes2, LANES)
    relaxed, part = call(
        functools.partial(coarse_and_last, size_x=size_x, size_y=size_y),
        [arr(own_x, own_y, nz), arr(8, LANES)],
        [window2] * 10 + [(LANES, LANES)] * 2 + [(8 * window1[1], LANES)]
        + [window1] * 9 + [(12 * 32, nz1)] + [window0] * 7 + [(12 * 32, nz)],
        yl1, own, yr1, w1, f1, yl, yr, own2, rim0, permit0, ion0, source0,
    )
    total = jnp.sum(sum_over(sum_over(part[:1], "gx"), "gy"))
    return relaxed, jnp.sqrt(total / (size_x * size_y * nz))


def solution(mesh):
    specs = (P("gx", "gy", None),) * 4
    return jax.shard_map(
        body, mesh=mesh, in_specs=specs, out_specs=(P("gx", "gy", None), P()), check_vma=False
    )
```

```python
import functools

import jax
import jax.numpy as jnp
from jax import lax
from jax.experimental import pallas as pl
from jax.experimental.pallas import tpu as pltpu
from jax.sharding import PartitionSpec as P

OMEGA = 0.8
LN2 = 0.6931471805599453
F32 = jnp.float32
LANES = 128
VMEM_LIMIT = 24 * 1024 * 1024

RIM_X0, RIM_Y0 = 3, 4
RIM_1 = 8
RIM_2 = 6


def roll(value, shift, axis):
    return pltpu.roll(value, shift % value.shape[axis], axis)


def iota(shape, dim):
    return lax.broadcasted_iota(jnp.int32, shape, dim)


def shared_matrix(rows, cols, ratio_rows, ratio_cols, value):
    match = iota((rows, cols), 0) // ratio_rows == iota((rows, cols), 1) // ratio_cols
    return jnp.where(match, value, 0.0).astype(F32)


def dot(left, right):
    return jnp.dot(left, right, precision=lax.Precision.HIGHEST, preferred_element_type=F32)


def dot_parts(left, right):
    high = left.astype(jnp.bfloat16)
    rest = left - high.astype(F32)
    middle = rest.astype(jnp.bfloat16)
    low = (rest - middle.astype(F32)).astype(jnp.bfloat16)
    parts = jnp.concatenate([low, middle, high], axis=1)
    return jnp.dot(parts, jnp.concatenate([right.astype(jnp.bfloat16)] * 3, axis=0), preferred_element_type=F32)


def low_half(shape):
    return iota(shape, 0) < 4


def shifted_tiles(first, second, left, right):
    low = low_half(first.shape)
    a, b = roll(first, 4, 0), roll(second, 4, 0)
    return jnp.where(low, left, a), jnp.where(low, a, b), jnp.where(low, b, right)


def row_mask(shape, first_row, last_row, origin, size, lanes=None):
    row = iota(shape, 0)
    place = row + origin
    good = (row >= first_row) & (row < last_row) & (place >= 0) & (place < size)
    if lanes is not None:
        good = good & (iota(shape, 1) < lanes)
    return jnp.where(good, 1.0, 0.0).astype(F32)


def inner_sides(shape):
    place, last = lax.axis_index("gy"), lax.axis_size("gy") - 1
    row = iota(shape, 0)
    return row >= jnp.where(place == 0, shape[0], 0), row >= jnp.where(place == last, shape[0], 0)


def plane_bar(place, size):
    return jnp.where((place >= 0) & (place < size), 0.5, 2.0).astype(F32)


def over_planes(first, last, step):
    def loop_body(x, carry):
        step(x)
        return carry

    lax.fori_loop(first, last, loop_body, 0, unroll=last - first)


def fill_weights(e_ref, weights, planes, scale, wrap_free):
    wx, wy, wz, wb, total = weights
    half = 0.5 * scale
    shape = e_ref.shape[1:]
    lane = iota(shape, 1)
    last = shape[1] - 1

    def along_x(x):
        wx[x] = half * (e_ref[x] + e_ref[x + 1])

    over_planes(0, planes - 1, along_x)

    def others(x):
        e = e_ref[x]
        y = half * (e + roll(e, -1, 0))
        z = half * (e + roll(e, -1, 1))
        if not wrap_free:
            z = jnp.where(lane < last, z, 0.0)
        faces = (wx[x] + wx[x - 1]) + (y + roll(y, 1, 0)) + (z + roll(z, 1, 1))
        if not wrap_free:
            b = jnp.where((lane == 0) | (lane == last), half * e, 0.0)
            wb[x] = b
            faces = faces + b
        wy[x] = y
        wz[x] = z
        total[x] = faces

    over_planes(1, planes - 1, others)


def flux_of(x, u_ref, weights):
    wx, wy, wz, wb, _ = weights
    u = u_ref[x]
    py = wy[x] * (roll(u, -1, 0) - u)
    pz = wz[x] * (roll(u, -1, 1) - u)
    flux = wx[x - 1] * (u - u_ref[x - 1]) - wx[x] * (u_ref[x + 1] - u)
    flux = flux + (roll(py, 1, 0) - py) + (roll(pz, 1, 1) - pz)
    if wb is not None:
        flux = flux + wb[x] * u
    return u, flux


def halves(u):
    return jnp.exp(u - LN2), jnp.exp(-u - LN2)


def sweep(u_ref, out_ref, weights, k_ref, f_ref, first, last, rows, origin, size):
    def step(x):
        u, flux = flux_of(x, u_ref, weights)
        up, down = halves(u)
        k = k_ref[x]
        defect = f_ref[x] - (flux + k * (up - down))
        slope = weights[4][x] + k * (up + down)
        moved = u + OMEGA * defect / slope
        out_ref[x] = jnp.where(rows > plane_bar(origin + x, size), moved, 0.0)

    over_planes(first, last, step)


def defect_at(x, u_ref, weights, k_ref, load):
    u, flux = flux_of(x, u_ref, weights)
    up, down = halves(u)
    return load - (flux + k_ref[x] * (up - down))


def pair_rows(ref, base, count=8):
    return ref[pl.ds(base, count, 2), :] + ref[pl.ds(base + 1, count, 2), :]


def rim_plane(x, brick, left, right, base, depth, rim):
    size = brick.shape[0]
    if x < rim:
        at = x - (rim - depth)
        return (left, base + at) if at >= 0 else None
    if x < rim + size:
        return (brick, x - rim)
    at = x - rim - size
    return (right, base + at) if at < depth else None


FINE_SENT = ((3, 0), (3, 3), (2, 6), (2, 8))


def fine_plane(x, index, brick, left, right):
    depth, base = FINE_SENT[index]
    return rim_plane(x, brick, left, right, base, depth, RIM_X0)


def tile_of(place, tile):
    if place is None:
        return None
    ref, x = place
    return ref[x, 8 * tile : 8 * tile + 8, :]


def pack_fine(s_ref, e_ref, k_ref, f_ref, xl_ref, xr_ref, up_ref, down_ref):
    bricks = (s_ref, e_ref, k_ref, f_ref)
    planes = s_ref.shape[0] + 2 * RIM_X0
    shape = (8, s_ref.shape[2])
    low = low_half(shape)
    zero = jnp.zeros(shape, F32)
    for x in range(planes):
        for pair in range(2):
            places = [fine_plane(x, 2 * pair + i, bricks[2 * pair + i], xl_ref, xr_ref) for i in range(2)]
            if places[0] is None:
                up_ref[pair, x] = zero
                down_ref[pair, x] = zero
                continue
            up_ref[pair, x] = jnp.where(low, roll(tile_of(places[0], 1), 4, 0), tile_of(places[1], 1))
            down_ref[pair, x] = jnp.where(low, tile_of(places[0], 0), roll(tile_of(places[1], 0), 4, 0))


def fine_first(
    s_ref, e_ref, k_ref, f_ref, xl_ref, xr_ref, yl_ref, yr_ref,
    stack_ref, u0_ref, kw_ref, fw_ref, wx, wy, wz, wb, total,
    ua, ub, ew_ref, gather, summed,
    *, size_x, size_y,
):
    bricks = (s_ref, e_ref, k_ref, f_ref)
    windows = (ua, ew_ref, kw_ref, fw_ref)
    own_x, own_y, nz = s_ref.shape
    planes = own_x + 2 * RIM_X0
    rows = own_y + 2 * RIM_Y0
    keep_left, keep_right = inner_sides((8, nz))
    for x in range(planes):
        for index in range(4):
            place = fine_plane(x, index, bricks[index], xl_ref, xr_ref)
            if place is None:
                windows[index][x] = jnp.zeros((rows, nz), F32)
                continue
            left = jnp.where(keep_left, yl_ref[index // 2, x], 0.0)
            right = jnp.where(keep_right, yr_ref[index // 2, x], 0.0)
            if index % 2 == 0:
                right = roll(right, 4, 0)
            else:
                left = roll(left, 4, 0)
            tiles = shifted_tiles(tile_of(place, 0), tile_of(place, 1), left, right)
            for i, tile in enumerate(tiles):
                windows[index][x, 8 * i : 8 * i + 8, :] = tile
    weights = (wx, wy, wz, wb, total)
    fill_weights(ew_ref, weights, planes, 1.0, False)
    origin_x = lax.axis_index("gx") * own_x - RIM_X0
    origin_y = lax.axis_index("gy") * own_y - RIM_Y0
    shape = (rows, nz)
    mask = row_mask(shape, 2, rows - 2, origin_y, size_y)
    sweep(ua, ub, weights, kw_ref, fw_ref, 1, planes - 1, mask, origin_x, size_x)
    mask = row_mask(shape, 3, rows - 3, origin_y, size_y)
    sweep(ub, ua, weights, kw_ref, fw_ref, 2, planes - 2, mask, origin_x, size_x)

    low = low_half((8, nz))
    pairs = own_x // 2

    def finish(j):
        x = RIM_X0 + 2 * j
        gather[pl.ds(j * rows, rows), :] = ua[x] + ua[x + 1]
        d = defect_at(x, ua, weights, kw_ref, fw_ref[x]) + defect_at(x + 1, ua, weights, kw_ref, fw_ref[x + 1])
        gather[pl.ds((pairs + j) * rows, rows), :] = d
        for i in range(2):
            u = ua[x + i]
            moved = [roll(u[8 * t : 8 * t + 8], 4, 0) for t in range(3)]
            u0_ref[2 * j + i, 0:8, :] = jnp.where(low, moved[0], moved[1])
            u0_ref[2 * j + i, 8:16, :] = jnp.where(low, moved[1], moved[2])

    over_planes(0, pairs, finish)
    base = 2 * pairs * rows
    for i, ref in enumerate((e_ref, k_ref)):
        for j in range(pairs):
            at = base + (i * pairs + j) * own_y
            gather[at : at + own_y, :] = ref[2 * j] + ref[2 * j + 1]
    summed[...] = dot(gather[...], shared_matrix(nz, nz // 2, 2, 1, 0.125))
    for j in range(pairs):
        stack_ref[0, j] = pair_rows(summed, base + j * own_y)
        stack_ref[1, j] = pair_rows(summed, base + (pairs + j) * own_y)
        stack_ref[2, j] = pair_rows(summed, j * rows + RIM_Y0)
        stack_ref[3, j] = pair_rows(summed, (pairs + j) * rows + RIM_Y0)


def middle_first(
    l_ref, o_ref, r_ref, u0_ref,
    up_ref, down_ref, stack_ref, w_ref, f_ref, k, v, wx, wy, wz, wb, total,
    e, wa, gather, summed,
    *, size_x, size_y,
):
    planes, own, nz = o_ref.shape[1:]
    rows = own + 2 * RIM_1
    shape = (rows, nz)
    keep_left, keep_right = inner_sides((own, nz))

    def joined(index, x):
        left = jnp.where(keep_left, l_ref[index, x], 0.0)
        right = jnp.where(keep_right, r_ref[index, x], 0.0)
        return jnp.concatenate([left, o_ref[index, x], right], axis=0)

    def assemble(x):
        e[x] = joined(0, x)
        k[x] = joined(1, x)
        v[x] = joined(2, x)

    over_planes(0, planes, assemble)
    weights = (wx, wy, wz, wb, total)
    fill_weights(e, weights, planes, 0.25, False)
    origin_x = lax.axis_index("gx") * own - RIM_1
    origin_y = lax.axis_index("gy") * own - RIM_1

    def load(x):
        f_ref[x] = defect_at(x, v, weights, k, joined(3, x))

    over_planes(2, planes - 2, load)
    mask = row_mask(shape, 2, rows - 2, origin_y, size_y)
    sweep(v, wa, weights, k, f_ref, 2, planes - 2, mask, origin_x, size_x)
    mask = row_mask(shape, 3, rows - 3, origin_y, size_y)
    sweep(wa, w_ref, weights, k, f_ref, 3, planes - 3, mask, origin_x, size_x)
    pairs = (planes - 8) // 2

    def finish(j):
        x = 4 + 2 * j
        d = defect_at(x, w_ref, weights, k, f_ref[x]) + defect_at(x + 1, w_ref, weights, k, f_ref[x + 1])
        at = pl.ds(j * rows, rows)
        gather[at, :nz] = e[x] + e[x + 1]
        gather[at, nz:] = k[x] + k[x + 1]
        at = pl.ds((pairs + j) * rows, rows)
        gather[at, :nz] = w_ref[x] + w_ref[x + 1]
        gather[at, nz:] = d

    over_planes(0, pairs, finish)
    summed[...] = dot(gather[...], shared_matrix(2 * nz, nz, 2, 1, 0.125))
    own_planes = u0_ref.shape[0]
    for a in range(2):
        for j in range(pairs):
            tile = pair_rows(summed, (a * pairs + j) * rows + 4)
            stack_ref[a, j] = tile
            if j < RIM_2:
                up_ref[a * RIM_2 + j] = tile
            if j >= pairs - RIM_2:
                down_ref[a * RIM_2 + j - (pairs - RIM_2)] = tile
    for x in range(RIM_X0):
        for t in range(4):
            rows_at, lanes_at = 8 * (t // 2), LANES * (t % 2)
            at = 2 * RIM_2 + 4 * x + t
            up_ref[at] = u0_ref[own_planes - RIM_X0 + x, rows_at : rows_at + 8, lanes_at : lanes_at + LANES]
            down_ref[at] = u0_ref[x, rows_at : rows_at + 8, lanes_at : lanes_at + LANES]


def pack_coarse(xl_ref, xr_ref, stack_ref, u0_ref, up_ref, down_ref, own_ref, rim_ref):
    spare = stack_ref.shape[1] // 2 - 2
    planes = 2 * RIM_2 + 4
    low = low_half((8, LANES))
    for a in range(2):
        for x in range(planes):
            if x < RIM_2:
                tile = xl_ref[a * RIM_2 + x]
            elif x < RIM_2 + 4:
                tile = stack_ref[a, x - RIM_2 + spare]
            else:
                tile = xr_ref[a * RIM_2 + x - RIM_2 - 4]
            at = a * planes + x
            own_ref[at] = tile
            up_ref[at] = tile
            down_ref[at] = tile
    own_planes = u0_ref.shape[0]
    base = 2 * RIM_2
    for x in range(own_planes + 2 * RIM_X0):
        if x < RIM_X0:
            tiles = [xl_ref[base + 4 * x + t] for t in range(4)]
        elif x < RIM_X0 + own_planes:
            tiles = [
                u0_ref[x - RIM_X0, 8 * (t // 2) : 8 * (t // 2) + 8, LANES * (t % 2) : LANES * (t % 2) + LANES]
                for t in range(4)
            ]
        else:
            tiles = [xr_ref[base + 4 * (x - RIM_X0 - own_planes) + t] for t in range(4)]
        at = 2 * planes + x
        up_ref[at] = jnp.where(low, roll(tiles[2], 4, 0), tiles[3])
        down_ref[at] = jnp.where(low, tiles[0], roll(tiles[1], 4, 0))
        for t in range(4):
            rim_ref[x, 8 * (t // 2) : 8 * (t // 2) + 8, LANES * (t % 2) : LANES * (t % 2) + LANES] = tiles[t]


def coarse_and_last(
    yl_ref, yr_ref, o2_ref, u0_ref,
    w1_ref, f1_ref, k1, v1_ref, wx1, wy1, wz1, wb1, t1,
    kw_ref, fw_ref, wx0, wy0, wz0, wb0, t0,
    out_ref, part_ref,
    e2, k2, v2, f2, a2, b2, wx2, wy2, wz2, t2, q2, s2, d2,
    a1, b1, d1, a0, b0, q0,
    *, size_x, size_y,
):
    place_x, place_y = lax.axis_index("gx"), lax.axis_index("gy")
    planes2 = 2 * RIM_2 + 4
    rows2 = planes2
    shape2 = (rows2, LANES)
    nz2 = LANES // 2
    row8 = iota((8, LANES), 0)
    inside = iota(shape2, 1) < nz2
    keep_left, keep_right = inner_sides((8, LANES))

    def window2(at):
        own = roll(o2_ref[at], 4, 0)
        upper = jnp.where(row8 >= 6, own, jnp.where(keep_left, yl_ref[at], 0.0))
        lower = jnp.where(row8 < 2, own, jnp.where(keep_right, yr_ref[at], 0.0))
        return jnp.concatenate([upper, lower], axis=0)

    def assemble2(x):
        both = window2(x)
        e2[x] = jnp.where(inside, both, 0.0)
        k2[x] = jnp.where(inside, roll(both, nz2, 1), 0.0)
        both = window2(planes2 + x)
        v2[x] = jnp.where(inside, both, 0.0)
        f2[x] = jnp.where(inside, roll(both, nz2, 1), 0.0)

    over_planes(0, planes2, assemble2)
    weights2 = (wx2, wy2, wz2, None, t2)
    fill_weights(e2, weights2, planes2, 0.0625, True)
    origin_x = place_x * 4 - RIM_2
    origin_y = place_y * 4 - RIM_2

    def load2(x):
        f2[x] = defect_at(x, v2, weights2, k2, f2[x])

    over_planes(1, planes2 - 1, load2)
    source = v2
    for i in range(4):
        target = a2 if i % 2 == 0 else b2
        mask = row_mask(shape2, 1 + i, rows2 - 1 - i, origin_y, size_y // 4, nz2)
        sweep(source, target, weights2, k2, f2, 1 + i, planes2 - 1 - i, mask, origin_x, size_x // 4)
        source = target
    for j in range(8):
        q2[16 * j : 16 * j + 16, :] = source[4 + j] - v2[4 + j]
    s2[...] = dot_parts(q2[...], shared_matrix(LANES, LANES, 1, 2, 1.0))
    planes1, rows1, nz1 = w1_ref.shape
    d2[...] = jnp.zeros(d2.shape, F32)
    for j in range(8):
        rows = roll(s2[16 * j : 16 * j + 16, :], -4, 0)[:8]
        d2[pl.ds(rows1 * j + 4, 8, 2), :] = rows
        d2[pl.ds(rows1 * j + 5, 8, 2), :] = rows

    own1 = planes1 - 2 * RIM_1
    shape1 = (rows1, nz1)
    weights1 = (wx1, wy1, wz1, wb1, t1)
    origin_x = place_x * own1 - RIM_1
    origin_y = place_y * own1 - RIM_1
    for x in range(4, 20):
        at = rows1 * ((x - 4) // 2)
        a1[x] = w1_ref[x] + d2[at : at + rows1, :]
    mask = row_mask(shape1, 5, rows1 - 5, origin_y, size_y // 2)
    sweep(a1, b1, weights1, k1, f1_ref, 5, planes1 - 5, mask, origin_x, size_x // 2)
    mask = row_mask(shape1, 6, rows1 - 6, origin_y, size_y // 2)
    sweep(b1, a1, weights1, k1, f1_ref, 6, planes1 - 6, mask, origin_x, size_x // 2)
    for j in range(12):
        rows = roll(a1[6 + j] - v1_ref[6 + j], -6, 0)[:16]
        d1[pl.ds(32 * j, 16, 2), :] = rows
        d1[pl.ds(32 * j + 1, 16, 2), :] = rows
    nz0 = 2 * nz1
    q0[...] = dot_parts(d1[...], shared_matrix(nz1, nz0, 1, 2, 1.0))

    own_x, own_y = out_ref.shape[:2]
    planes0 = own_x + 2 * RIM_X0
    rows0 = own_y + 2 * RIM_Y0
    shape0 = (rows0, nz0)
    base = 2 * planes2
    for x in range(planes0):
        left = jnp.where(keep_left, yl_ref[base + x], 0.0)
        right = jnp.where(keep_right, yr_ref[base + x], 0.0)
        left = jnp.concatenate([left, roll(left, 4, 0)], axis=1)
        right = jnp.concatenate([roll(right, 4, 0), right], axis=1)
        tiles = shifted_tiles(u0_ref[x, 0:8, :], u0_ref[x, 8:16, :], left, right)
        at = 32 * ((x + 1) // 2)
        for i, tile in enumerate(tiles):
            a0[x, 8 * i : 8 * i + 8, :] = tile + q0[at + 8 * i : at + 8 * i + 8, :]
    weights0 = (wx0, wy0, wz0, wb0, t0)
    origin_x = place_x * own_x - RIM_X0
    origin_y = place_y * own_y - RIM_Y0
    mask = row_mask(shape0, 2, rows0 - 2, origin_y, size_y)
    sweep(a0, b0, weights0, kw_ref, fw_ref, 1, planes0 - 1, mask, origin_x, size_x)
    mask = row_mask(shape0, 3, rows0 - 3, origin_y, size_y)
    sweep(b0, a0, weights0, kw_ref, fw_ref, 2, planes0 - 2, mask, origin_x, size_x)
    low = low_half((8, nz0))

    def finish(x, acc):
        d = defect_at(x, a0, weights0, kw_ref, fw_ref[x])
        u = a0[x]
        moved = [roll(u[8 * t : 8 * t + 8], 4, 0) for t in range(3)]
        out_ref[x - RIM_X0, 0:8, :] = jnp.where(low, moved[0], moved[1])
        out_ref[x - RIM_X0, 8:16, :] = jnp.where(low, moved[1], moved[2])
        return acc + d * d

    acc = lax.fori_loop(RIM_X0, RIM_X0 + own_x, finish, jnp.zeros(shape0, F32), unroll=own_x)
    row = iota(shape0, 0)
    acc = jnp.where((row >= RIM_Y0) & (row < RIM_Y0 + own_y), acc, 0.0)
    acc = jnp.sum(acc, axis=0, keepdims=True)
    acc = jnp.sum(acc, axis=1, keepdims=True)
    part_ref[...] = jnp.broadcast_to(acc, part_ref.shape)


def arr(*shape):
    return jax.ShapeDtypeStruct(shape, F32)


def call(kernel, outs, scratch, *args):
    return pl.pallas_call(
        kernel,
        out_shape=outs,
        in_specs=[pl.BlockSpec(memory_space=pltpu.VMEM)] * len(args),
        out_specs=[pl.BlockSpec(memory_space=pltpu.VMEM)] * len(outs),
        scratch_shapes=[pltpu.VMEM(shape, F32) for shape in scratch],
        compiler_params=pltpu.CompilerParams(vmem_limit_bytes=VMEM_LIMIT),
    )(*args)


def swap(upward, downward, axis, ring=False):
    size = lax.axis_size(axis)
    up = [(i, (i + 1) % size) for i in range(size if ring else size - 1)]
    down = [(j, i) for i, j in up]
    return lax.ppermute(upward, axis, up), lax.ppermute(downward, axis, down)


def sum_over(part, axis):
    size = lax.axis_size(axis)
    rows = jnp.broadcast_to(part, (size, LANES))
    return jnp.sum(lax.all_to_all(rows, axis, 0, 0, tiled=True), axis=0, keepdims=True)


def body(start, permit, ion, source):
    own_x, own_y, nz = start.shape
    size_x, size_y = own_x * lax.axis_size("gx"), own_y * lax.axis_size("gy")
    planes0, rows0 = own_x + 2 * RIM_X0, own_y + 2 * RIM_Y0
    window0 = (planes0, rows0, nz)

    fields = (start, permit, ion, source)
    depths = [depth for depth, _ in FINE_SENT]
    upward = jnp.concatenate([a[own_x - d :] for a, d in zip(fields, depths)], axis=0)
    downward = jnp.concatenate([a[:d] for a, d in zip(fields, depths)], axis=0)
    xl, xr = swap(upward, downward, "gx")
    packed = arr(2, planes0, 8, nz)
    upward, downward = call(pack_fine, [packed, packed], [], *fields, xl, xr)
    yl, yr = swap(upward, downward, "gy", True)
    own1, own1_y, nz1 = own_x // 2, own_y // 2, nz // 2
    gathered = 2 * own1 * rows0 + 2 * own1 * own_y
    stack1, u0, *level0 = call(
        functools.partial(fine_first, size_x=size_x, size_y=size_y),
        [arr(4, own1, own1_y, nz1), arr(own_x, own_y, nz)] + [arr(*window0)] * 7,
        [window0] * 3 + [(gathered, nz), (gathered, nz1)],
        *fields, xl, xr, yl, yr,
    )

    xl, xr = swap(stack1, stack1, "gx")
    own = jnp.concatenate([xl, stack1, xr], axis=1)
    yl1, yr1 = swap(own, own, "gy", True)
    planes1 = own1 + 2 * RIM_1
    window1 = (planes1, own1_y + 2 * RIM_1, nz1)
    sent_x = 2 * RIM_2 + 4 * RIM_X0
    upward, downward, stack2, *level1 = call(
        functools.partial(middle_first, size_x=size_x // 2, size_y=size_y // 2),
        [arr(sent_x, 8, LANES)] * 2 + [arr(2, 8, 8, LANES)] + [arr(*window1)] * 9,
        [window1] * 2 + [(16 * window1[1], 2 * nz1), (16 * window1[1], nz1)],
        yl1, own, yr1, u0,
    )

    xl, xr = swap(upward, downward, "gx")
    planes2 = 2 * RIM_2 + 4
    sent_y = 2 * planes2 + planes0
    upward, downward, own2, rim0 = call(
        pack_coarse,
        [arr(sent_y, 8, LANES)] * 2 + [arr(2 * planes2, 8, LANES), arr(planes0, own_y, nz)],
        [], xl, xr, stack2, u0,
    )
    yl, yr = swap(upward, downward, "gy", True)
    window2 = (planes2, planes2, LANES)
    relaxed, part = call(
        functools.partial(coarse_and_last, size_x=size_x, size_y=size_y),
        [arr(own_x, own_y, nz), arr(8, LANES)],
        [window2] * 10 + [(LANES, LANES)] * 2 + [(8 * window1[1], LANES)]
        + [window1] * 2 + [(12 * 32, nz1)] + [window0] * 2 + [(12 * 32, nz)],
        yl, yr, own2, rim0, *level1, *level0,
    )
    total = sum_over(sum_over(part[:1], "gx"), "gy")[0, 0]
    return relaxed, jnp.sqrt(total / (size_x * size_y * nz))


def solution(mesh):
    specs = (P("gx", "gy", None),) * 4
    return jax.shard_map(
        body, mesh=mesh, in_specs=specs, out_specs=(P("gx", "gy", None), P()), check_vma=False
    )
```

```python
import functools

import jax
import jax.numpy as jnp
from jax import lax
from jax.experimental import pallas as pl
from jax.experimental.pallas import tpu as pltpu
from jax.sharding import PartitionSpec as P

OMEGA = 0.8
LN2 = 0.6931471805599453
F32 = jnp.float32
LANES = 128
VMEM_LIMIT = 24 * 1024 * 1024
AT_ONCE_0, AT_ONCE_1, AT_ONCE_2 = 1, 3, 7

RIM_X0, RIM_Y0 = 3, 4
RIM_1 = 8
RIM_2 = 6


def roll(value, shift, axis):
    return pltpu.roll(value, shift % value.shape[axis], axis)


def iota(shape, dim):
    return lax.broadcasted_iota(jnp.int32, shape, dim)


def shared_matrix(rows, cols, ratio_rows, ratio_cols, value):
    match = iota((rows, cols), 0) // ratio_rows == iota((rows, cols), 1) // ratio_cols
    return jnp.where(match, value, 0.0).astype(F32)


def dot(left, right):
    return jnp.dot(left, right, precision=lax.Precision.HIGHEST, preferred_element_type=F32)


def dot_parts(left, right):
    high = left.astype(jnp.bfloat16)
    rest = left - high.astype(F32)
    middle = rest.astype(jnp.bfloat16)
    low = (rest - middle.astype(F32)).astype(jnp.bfloat16)
    parts = jnp.concatenate([low, middle, high], axis=1)
    return jnp.dot(parts, jnp.concatenate([right.astype(jnp.bfloat16)] * 3, axis=0), preferred_element_type=F32)


def low_half(shape):
    return iota(shape, 0) < 4


def shifted_tiles(first, second, left, right):
    low = low_half(first.shape)
    a, b = roll(first, 4, 0), roll(second, 4, 0)
    return jnp.where(low, left, a), jnp.where(low, a, b), jnp.where(low, b, right)


def row_mask(shape, first_row, last_row, origin, size, lanes=None):
    row = iota(shape, 0)
    place = row + origin
    good = (row >= first_row) & (row < last_row) & (place >= 0) & (place < size)
    if lanes is not None:
        good = good & (iota(shape, 1) < lanes)
    return jnp.where(good, 1.0, 0.0).astype(F32)


def inner_sides(shape):
    place, last = lax.axis_index("gy"), lax.axis_size("gy") - 1
    row = iota(shape, 0)
    return row >= jnp.where(place == 0, shape[0], 0), row >= jnp.where(place == last, shape[0], 0)


def plane_bar(place, size):
    return jnp.where((place >= 0) & (place < size), 0.5, 2.0).astype(F32)


def over_planes(first, last, step):
    def loop_body(x, carry):
        step(x)
        return carry

    lax.fori_loop(first, last, loop_body, 0, unroll=last - first)


def fill_weights(e_ref, weights, planes, scale, wrap_free, first=0):
    wx, wy, wz, wb, total = weights
    half = 0.5 * scale
    shape = e_ref.shape[1:]
    lane = iota(shape, 1)
    last = shape[1] - 1

    def along_x(x):
        wx[x] = half * (e_ref[x] + e_ref[x + 1])

    over_planes(first, planes - 1 - first, along_x)

    def others(x):
        e = e_ref[x]
        y = half * (e + roll(e, -1, 0))
        z = half * (e + roll(e, -1, 1))
        if not wrap_free:
            z = jnp.where(lane < last, z, 0.0)
        faces = (wx[x] + wx[x - 1]) + (y + roll(y, 1, 0)) + (z + roll(z, 1, 1))
        if not wrap_free:
            b = jnp.where((lane == 0) | (lane == last), half * e, 0.0)
            wb[x] = b
            faces = faces + b
        wy[x] = y
        wz[x] = z
        total[x] = faces

    over_planes(first + 1, planes - 1 - first, others)


def planes_at(ref, x, count):
    if count == 1:
        return ref[x]
    return ref[x : x + count].reshape(count * ref.shape[1], ref.shape[2])


def runs(first, last, count):
    return [(x, min(count, last - x)) for x in range(first, last, count)]


def flux_of(x, u_ref, weights, count=1):
    wx, wy, wz, wb, _ = weights
    u = planes_at(u_ref, x, count)
    py = planes_at(wy, x, count) * (roll(u, -1, 0) - u)
    pz = planes_at(wz, x, count) * (roll(u, -1, 1) - u)
    flux = planes_at(wx, x - 1, count) * (u - planes_at(u_ref, x - 1, count))
    flux = flux - planes_at(wx, x, count) * (planes_at(u_ref, x + 1, count) - u)
    flux = flux + (roll(py, 1, 0) - py) + (roll(pz, 1, 1) - pz)
    if wb is not None:
        flux = flux + planes_at(wb, x, count) * u
    return u, flux


def halves(u):
    return jnp.exp(u - LN2), jnp.exp(-u - LN2)


def sweep(u_ref, out_ref, weights, k_ref, f_ref, first, last, rows, origin, size, at_once=1):
    height = u_ref.shape[1]
    for x, count in runs(first, last, at_once):
        u, flux = flux_of(x, u_ref, weights, count)
        up, down = halves(u)
        k = planes_at(k_ref, x, count)
        defect = planes_at(f_ref, x, count) - (flux + k * (up - down))
        slope = planes_at(weights[4], x, count) + k * (up + down)
        moved = u + OMEGA * defect / slope
        for i in range(count):
            plane = moved[i * height : (i + 1) * height]
            out_ref[x + i] = jnp.where(rows > plane_bar(origin + x + i, size), plane, 0.0)


def defect_at(x, u_ref, weights, k_ref, load, count=1):
    u, flux = flux_of(x, u_ref, weights, count)
    up, down = halves(u)
    return load - (flux + planes_at(k_ref, x, count) * (up - down))


def defects(u_ref, weights, k_ref, f_ref, first, last, at_once):
    height = u_ref.shape[1]
    for x, count in runs(first, last, at_once):
        d = defect_at(x, u_ref, weights, k_ref, planes_at(f_ref, x, count), count)
        for i in range(count):
            f_ref[x + i] = d[i * height : (i + 1) * height]


def pair_rows(ref, base, count=8):
    return ref[pl.ds(base, count, 2), :] + ref[pl.ds(base + 1, count, 2), :]


def rim_plane(x, brick, left, right, base, depth, rim):
    size = brick.shape[0]
    if x < rim:
        at = x - (rim - depth)
        return (left, base + at) if at >= 0 else None
    if x < rim + size:
        return (brick, x - rim)
    at = x - rim - size
    return (right, base + at) if at < depth else None


FINE_SENT = ((3, 0), (3, 3), (2, 6), (2, 8))


def fine_plane(x, index, brick, left, right):
    depth, base = FINE_SENT[index]
    return rim_plane(x, brick, left, right, base, depth, RIM_X0)


def tile_of(place, tile):
    if place is None:
        return None
    ref, x = place
    return ref[x, 8 * tile : 8 * tile + 8, :]


def pack_fine(bricks, planes, up_ref, down_ref):
    low = low_half(up_ref.shape[2:])
    for at, sources in enumerate(planes):
        for pair in range(2):
            first, second = (place(bricks) for place in sources[2 * pair : 2 * pair + 2])
            if first is None:
                up_ref[pair, at] = jnp.zeros(up_ref.shape[2:], F32)
                down_ref[pair, at] = jnp.zeros(up_ref.shape[2:], F32)
                continue
            up_ref[pair, at] = jnp.where(low, roll(tile_of(first, 1), 4, 0), tile_of(second, 1))
            down_ref[pair, at] = jnp.where(low, tile_of(first, 0), roll(tile_of(second, 0), 4, 0))


def pack_fine_own(s_ref, e_ref, k_ref, f_ref, up_ref, down_ref):
    planes = [
        [functools.partial(lambda refs, i, x: (refs[i], x), i=i, x=x) for i in range(4)]
        for x in range(s_ref.shape[0])
    ]
    pack_fine((s_ref, e_ref, k_ref, f_ref), planes, up_ref, down_ref)


def rim_planes(own):
    return list(range(RIM_X0)) + list(range(RIM_X0 + own, RIM_X0 + own + RIM_X0))


def pack_fine_rim(xl_ref, xr_ref, up_ref, down_ref):
    own = xl_ref.shape[1]
    brick = jax.ShapeDtypeStruct((own,), F32)
    planes = [
        [functools.partial(lambda refs, i, x: fine_plane(x, i, brick, *refs), i=i, x=x) for i in range(4)]
        for x in rim_planes(own)
    ]
    pack_fine((xl_ref, xr_ref), planes, up_ref, down_ref)


def hand_on(in_ref, out_ref):
    out_ref[...] = in_ref[...]


def join_rims(xl_ref, xr_ref, yl_ref, yr_ref, rim_ref):
    del yl_ref, yr_ref
    planes = xl_ref.shape[1]
    rim_ref[:, :planes] = xl_ref[...]
    rim_ref[:, planes:] = xr_ref[...]


def fine_first(
    s_ref, e_ref, k_ref, f_ref, xl_ref, xr_ref, yl_ref, yr_ref, cl_ref, cr_ref,
    up_ref, down_ref, stack_ref, u0_ref, kw_ref, fw_ref, wx, wy, wz, wb, total,
    ua, ub, ew_ref, gather, summed,
    *, size_x, size_y,
):
    bricks = (s_ref, e_ref, k_ref, f_ref)
    windows = (ua, ew_ref, kw_ref, fw_ref)
    own_x, own_y, nz = s_ref.shape
    planes = own_x + 2 * RIM_X0
    rows = own_y + 2 * RIM_Y0
    keep_left, keep_right = inner_sides((8, nz))
    corners = rim_planes(own_x)
    for x in range(planes):
        if x in corners:
            l_ref, r_ref, at = cl_ref, cr_ref, corners.index(x)
        else:
            l_ref, r_ref, at = yl_ref, yr_ref, x - RIM_X0
        for index in range(4):
            place = fine_plane(x, index, bricks[index], xl_ref, xr_ref)
            if place is None:
                windows[index][x] = jnp.zeros((rows, nz), F32)
                continue
            left = jnp.where(keep_left, l_ref[index // 2, at], 0.0)
            right = jnp.where(keep_right, r_ref[index // 2, at], 0.0)
            if index % 2 == 0:
                right = roll(right, 4, 0)
            else:
                left = roll(left, 4, 0)
            tiles = shifted_tiles(tile_of(place, 0), tile_of(place, 1), left, right)
            for i, tile in enumerate(tiles):
                windows[index][x, 8 * i : 8 * i + 8, :] = tile
    weights = (wx, wy, wz, wb, total)
    fill_weights(ew_ref, weights, planes, 1.0, False)
    origin_x = lax.axis_index("gx") * own_x - RIM_X0
    origin_y = lax.axis_index("gy") * own_y - RIM_Y0
    shape = (rows, nz)
    mask = row_mask(shape, 2, rows - 2, origin_y, size_y)
    sweep(ua, ub, weights, kw_ref, fw_ref, 1, planes - 1, mask, origin_x, size_x, AT_ONCE_0)
    mask = row_mask(shape, 3, rows - 3, origin_y, size_y)
    sweep(ub, ua, weights, kw_ref, fw_ref, 2, planes - 2, mask, origin_x, size_x, AT_ONCE_0)

    low = low_half((8, nz))
    pairs = own_x // 2

    def finish(j):
        x = RIM_X0 + 2 * j
        gather[pl.ds(j * rows, rows), :] = ua[x] + ua[x + 1]
        d = defect_at(x, ua, weights, kw_ref, fw_ref[x]) + defect_at(x + 1, ua, weights, kw_ref, fw_ref[x + 1])
        gather[pl.ds((pairs + j) * rows, rows), :] = d
        for i in range(2):
            u = ua[x + i]
            moved = [roll(u[8 * t : 8 * t + 8], 4, 0) for t in range(3)]
            u0_ref[2 * j + i, 0:8, :] = jnp.where(low, moved[0], moved[1])
            u0_ref[2 * j + i, 8:16, :] = jnp.where(low, moved[1], moved[2])

    over_planes(0, pairs, finish)
    base = 2 * pairs * rows
    for i, ref in enumerate((e_ref, k_ref)):
        for j in range(pairs):
            at = base + (i * pairs + j) * own_y
            gather[at : at + own_y, :] = ref[2 * j] + ref[2 * j + 1]
    summed[...] = dot(gather[...], shared_matrix(nz, nz // 2, 2, 1, 0.125))
    for j in range(pairs):
        tiles = (
            pair_rows(summed, base + j * own_y),
            pair_rows(summed, base + (pairs + j) * own_y),
            pair_rows(summed, j * rows + RIM_Y0),
            pair_rows(summed, (pairs + j) * rows + RIM_Y0),
        )
        for index, tile in enumerate(tiles):
            stack_ref[index, j] = tile
            if j > 0:
                up_ref[index, j - 1] = tile
            if j < pairs - 1:
                down_ref[index, j] = tile


def middle_first(
    o_ref, xl_ref, xr_ref, yl_ref, yr_ref, cl_ref, cr_ref, u0_ref,
    up_ref, down_ref, y_up_ref, y_down_ref, stack_ref, w_ref, f_ref, k, v, wx, wy, wz, wb, total,
    e, wa, gather, summed,
    *, size_x, size_y,
):
    own, nz = o_ref.shape[2:]
    planes = own + 2 * RIM_1
    rows = own + 2 * RIM_1
    shape = (rows, nz)
    keep_left, keep_right = inner_sides((own, nz))
    sent = RIM_1 - 1

    def assemble(x, middle, left, right, at, side):
        for index, ref in enumerate((e, k, v, f_ref)):
            lower = jnp.where(keep_left, left[index, side], 0.0)
            upper = jnp.where(keep_right, right[index, side], 0.0)
            ref[x] = jnp.concatenate([lower, middle[index, at], upper], axis=0)

    for x in range(1, planes - 1):
        if x < RIM_1:
            assemble(x, xl_ref, cl_ref, cr_ref, x - 1, x - 1)
        elif x < RIM_1 + own:
            assemble(x, o_ref, yl_ref, yr_ref, x - RIM_1, x - RIM_1)
        else:
            assemble(x, xr_ref, cl_ref, cr_ref, x - RIM_1 - own, sent + x - RIM_1 - own)
    weights = (wx, wy, wz, wb, total)
    fill_weights(e, weights, planes, 0.25, False, 1)
    origin_x = lax.axis_index("gx") * own - RIM_1
    origin_y = lax.axis_index("gy") * own - RIM_1

    defects(v, weights, k, f_ref, 2, planes - 2, AT_ONCE_1)
    mask = row_mask(shape, 2, rows - 2, origin_y, size_y)
    sweep(v, wa, weights, k, f_ref, 2, planes - 2, mask, origin_x, size_x, AT_ONCE_1)
    mask = row_mask(shape, 3, rows - 3, origin_y, size_y)
    sweep(wa, w_ref, weights, k, f_ref, 3, planes - 3, mask, origin_x, size_x, AT_ONCE_1)
    pairs = (planes - 8) // 2

    def finish(j):
        x = 4 + 2 * j
        d = defect_at(x, w_ref, weights, k, f_ref[x]) + defect_at(x + 1, w_ref, weights, k, f_ref[x + 1])
        at = pl.ds(j * rows, rows)
        gather[at, :nz] = e[x] + e[x + 1]
        gather[at, nz:] = k[x] + k[x + 1]
        at = pl.ds((pairs + j) * rows, rows)
        gather[at, :nz] = w_ref[x] + w_ref[x + 1]
        gather[at, nz:] = d

    over_planes(0, pairs, finish)
    summed[...] = dot(gather[...], shared_matrix(2 * nz, nz, 2, 1, 0.125))
    for a in range(2):
        for j in range(pairs):
            tile = pair_rows(summed, (a * pairs + j) * rows + 4)
            stack_ref[a, j] = tile
            if j < RIM_2:
                up_ref[a * RIM_2 + j] = tile
            if j >= pairs - RIM_2:
                down_ref[a * RIM_2 + j - (pairs - RIM_2)] = tile
    for a in range(2):
        for x in range(4):
            tile = stack_ref[a, pairs // 2 - 2 + x]
            y_up_ref[4 * a + x] = tile
            y_down_ref[4 * a + x] = tile
    own_planes = u0_ref.shape[0]
    for x in range(own_planes):
        tiles = quarter_tiles(u0_ref, x)
        y_up_ref[8 + x], y_down_ref[8 + x] = pack_rows(tiles)
        for t in range(4):
            if x < RIM_X0:
                down_ref[2 * RIM_2 + 4 * x + t] = tiles[t]
            if x >= own_planes - RIM_X0:
                up_ref[2 * RIM_2 + 4 * (x - own_planes + RIM_X0) + t] = tiles[t]


def quarter_tiles(ref, x):
    return [ref[x, 8 * (t // 2) : 8 * (t // 2) + 8, LANES * (t % 2) : LANES * (t % 2) + LANES] for t in range(4)]


def pack_rows(tiles):
    low = low_half(tiles[0].shape)
    last = jnp.where(low, roll(tiles[2], 4, 0), tiles[3])
    return last, jnp.where(low, tiles[0], roll(tiles[1], 4, 0))


def pack_coarse(xl_ref, xr_ref, yl_ref, yr_ref, up_ref, down_ref):
    del yl_ref, yr_ref
    for a in range(2):
        for x in range(2 * RIM_2):
            tile = xl_ref[a * RIM_2 + x] if x < RIM_2 else xr_ref[a * RIM_2 + x - RIM_2]
            up_ref[2 * RIM_2 * a + x] = tile
            down_ref[2 * RIM_2 * a + x] = tile
    for x in range(2 * RIM_X0):
        ref, at = (xl_ref, x) if x < RIM_X0 else (xr_ref, x - RIM_X0)
        tiles = [ref[2 * RIM_2 + 4 * at + t] for t in range(4)]
        up_ref[4 * RIM_2 + x], down_ref[4 * RIM_2 + x] = pack_rows(tiles)


def coarse_and_last(
    xl_ref, xr_ref, yl_ref, yr_ref, cl_ref, cr_ref, o2_ref, u0_ref,
    w1_ref, f1_ref, k1, v1_ref, wx1, wy1, wz1, wb1, t1,
    kw_ref, fw_ref, wx0, wy0, wz0, wb0, t0,
    out_ref, part_ref,
    e2, k2, v2, f2, a2, b2, wx2, wy2, wz2, t2, q2, s2, d2,
    a1, b1, d1, a0, b0, q0,
    *, size_x, size_y,
):
    place_x, place_y = lax.axis_index("gx"), lax.axis_index("gy")
    planes2 = 2 * RIM_2 + 4
    rows2 = planes2
    shape2 = (rows2, LANES)
    nz2 = LANES // 2
    row8 = iota((8, LANES), 0)
    inside = iota(shape2, 1) < nz2
    keep_left, keep_right = inner_sides((8, LANES))

    spare = o2_ref.shape[1] // 2 - 2

    def window2(a, x):
        if x < RIM_2:
            own, at = xl_ref[a * RIM_2 + x], 2 * RIM_2 * a + x
            left, right = cl_ref[at], cr_ref[at]
        elif x < RIM_2 + 4:
            own, at = o2_ref[a, spare + x - RIM_2], 4 * a + x - RIM_2
            left, right = yl_ref[at], yr_ref[at]
        else:
            own, at = xr_ref[a * RIM_2 + x - RIM_2 - 4], 2 * RIM_2 * a + x - 4
            left, right = cl_ref[at], cr_ref[at]
        own = roll(own, 4, 0)
        upper = jnp.where(row8 >= 6, own, jnp.where(keep_left, left, 0.0))
        lower = jnp.where(row8 < 2, own, jnp.where(keep_right, right, 0.0))
        return jnp.concatenate([upper, lower], axis=0)

    for x in range(planes2):
        both = window2(0, x)
        e2[x] = jnp.where(inside, both, 0.0)
        k2[x] = jnp.where(inside, roll(both, nz2, 1), 0.0)
        both = window2(1, x)
        v2[x] = jnp.where(inside, both, 0.0)
        f2[x] = jnp.where(inside, roll(both, nz2, 1), 0.0)

    weights2 = (wx2, wy2, wz2, None, t2)
    fill_weights(e2, weights2, planes2, 0.0625, True)
    origin_x = place_x * 4 - RIM_2
    origin_y = place_y * 4 - RIM_2

    defects(v2, weights2, k2, f2, 1, planes2 - 1, AT_ONCE_2)
    source = v2
    for i in range(4):
        target = a2 if i % 2 == 0 else b2
        mask = row_mask(shape2, 1 + i, rows2 - 1 - i, origin_y, size_y // 4, nz2)
        last = planes2 - 1 - i
        sweep(source, target, weights2, k2, f2, 1 + i, last, mask, origin_x, size_x // 4, AT_ONCE_2)
        source = target
    for j in range(8):
        q2[16 * j : 16 * j + 16, :] = source[4 + j] - v2[4 + j]
    s2[...] = dot_parts(q2[...], shared_matrix(LANES, LANES, 1, 2, 1.0))
    planes1, rows1, nz1 = w1_ref.shape
    d2[...] = jnp.zeros(d2.shape, F32)
    for j in range(8):
        rows = roll(s2[16 * j : 16 * j + 16, :], -4, 0)[:8]
        d2[pl.ds(rows1 * j + 4, 8, 2), :] = rows
        d2[pl.ds(rows1 * j + 5, 8, 2), :] = rows

    own1 = planes1 - 2 * RIM_1
    shape1 = (rows1, nz1)
    weights1 = (wx1, wy1, wz1, wb1, t1)
    origin_x = place_x * own1 - RIM_1
    origin_y = place_y * own1 - RIM_1
    for x in range(4, 20):
        at = rows1 * ((x - 4) // 2)
        a1[x] = w1_ref[x] + d2[at : at + rows1, :]
    mask = row_mask(shape1, 5, rows1 - 5, origin_y, size_y // 2)
    sweep(a1, b1, weights1, k1, f1_ref, 5, planes1 - 5, mask, origin_x, size_x // 2, AT_ONCE_1)
    mask = row_mask(shape1, 6, rows1 - 6, origin_y, size_y // 2)
    sweep(b1, a1, weights1, k1, f1_ref, 6, planes1 - 6, mask, origin_x, size_x // 2, AT_ONCE_1)
    for j in range(12):
        rows = roll(a1[6 + j] - v1_ref[6 + j], -6, 0)[:16]
        d1[pl.ds(32 * j, 16, 2), :] = rows
        d1[pl.ds(32 * j + 1, 16, 2), :] = rows
    nz0 = 2 * nz1
    q0[...] = dot_parts(d1[...], shared_matrix(nz1, nz0, 1, 2, 1.0))

    own_x, own_y = out_ref.shape[:2]
    planes0 = own_x + 2 * RIM_X0
    rows0 = own_y + 2 * RIM_Y0
    shape0 = (rows0, nz0)
    corners = rim_planes(own_x)
    for x in range(planes0):
        if x in corners:
            at = corners.index(x)
            ref, first = (xl_ref, at) if x < RIM_X0 else (xr_ref, at - RIM_X0)
            tiles = [ref[2 * RIM_2 + 4 * first + t] for t in range(4)]
            left, right = cl_ref[4 * RIM_2 + at], cr_ref[4 * RIM_2 + at]
        else:
            tiles = quarter_tiles(u0_ref, x - RIM_X0)
            left, right = yl_ref[8 + x - RIM_X0], yr_ref[8 + x - RIM_X0]
        upper = jnp.concatenate(tiles[:2], axis=1)
        lower = jnp.concatenate(tiles[2:], axis=1)
        left = jnp.where(keep_left, left, 0.0)
        right = jnp.where(keep_right, right, 0.0)
        left = jnp.concatenate([left, roll(left, 4, 0)], axis=1)
        right = jnp.concatenate([roll(right, 4, 0), right], axis=1)
        tiles = shifted_tiles(upper, lower, left, right)
        at = 32 * ((x + 1) // 2)
        for i, tile in enumerate(tiles):
            a0[x, 8 * i : 8 * i + 8, :] = tile + q0[at + 8 * i : at + 8 * i + 8, :]
    weights0 = (wx0, wy0, wz0, wb0, t0)
    origin_x = place_x * own_x - RIM_X0
    origin_y = place_y * own_y - RIM_Y0
    mask = row_mask(shape0, 2, rows0 - 2, origin_y, size_y)
    sweep(a0, b0, weights0, kw_ref, fw_ref, 1, planes0 - 1, mask, origin_x, size_x, AT_ONCE_0)
    mask = row_mask(shape0, 3, rows0 - 3, origin_y, size_y)
    sweep(b0, a0, weights0, kw_ref, fw_ref, 2, planes0 - 2, mask, origin_x, size_x, AT_ONCE_0)
    low = low_half((8, nz0))

    def finish(x, acc):
        d = defect_at(x, a0, weights0, kw_ref, fw_ref[x])
        u = a0[x]
        moved = [roll(u[8 * t : 8 * t + 8], 4, 0) for t in range(3)]
        out_ref[x - RIM_X0, 0:8, :] = jnp.where(low, moved[0], moved[1])
        out_ref[x - RIM_X0, 8:16, :] = jnp.where(low, moved[1], moved[2])
        return acc + d * d

    acc = lax.fori_loop(RIM_X0, RIM_X0 + own_x, finish, jnp.zeros(shape0, F32), unroll=own_x)
    row = iota(shape0, 0)
    acc = jnp.where((row >= RIM_Y0) & (row < RIM_Y0 + own_y), acc, 0.0)
    acc = jnp.sum(acc, axis=0, keepdims=True)
    acc = jnp.sum(acc, axis=1, keepdims=True)
    part_ref[...] = jnp.broadcast_to(acc, part_ref.shape)


def arr(*shape):
    return jax.ShapeDtypeStruct(shape, F32)


def call(kernel, outs, scratch, *args):
    return pl.pallas_call(
        kernel,
        out_shape=outs,
        in_specs=[pl.BlockSpec(memory_space=pltpu.VMEM)] * len(args),
        out_specs=[pl.BlockSpec(memory_space=pltpu.VMEM)] * len(outs),
        scratch_shapes=[pltpu.VMEM(shape, F32) for shape in scratch],
        compiler_params=pltpu.CompilerParams(vmem_limit_bytes=VMEM_LIMIT),
    )(*args)


def swap(upward, downward, axis, ring=False):
    size = lax.axis_size(axis)
    up = [(i, (i + 1) % size) for i in range(size if ring else size - 1)]
    down = [(j, i) for i, j in up]
    return lax.ppermute(upward, axis, up), lax.ppermute(downward, axis, down)


def sum_over(part, axis):
    size = lax.axis_size(axis)
    rows = jnp.broadcast_to(part, (size, LANES))
    return jnp.sum(lax.all_to_all(rows, axis, 0, 0, tiled=True), axis=0, keepdims=True)


def body(start, permit, ion, source):
    own_x, own_y, nz = start.shape
    size_x, size_y = own_x * lax.axis_size("gx"), own_y * lax.axis_size("gy")
    planes0, rows0 = own_x + 2 * RIM_X0, own_y + 2 * RIM_Y0
    window0 = (planes0, rows0, nz)

    fields = (start, permit, ion, source)
    depths = [depth for depth, _ in FINE_SENT]
    upward = jnp.concatenate([a[own_x - d :] for a, d in zip(fields, depths)], axis=0)
    downward = jnp.concatenate([a[:d] for a, d in zip(fields, depths)], axis=0)
    xl, xr = swap(upward, downward, "gx")
    yl, yr = swap(*call(pack_fine_own, [arr(2, own_x, 8, nz)] * 2, [], *fields), "gy", True)
    cl, cr = swap(*call(pack_fine_rim, [arr(2, 2 * RIM_X0, 8, nz)] * 2, [], xl, xr), "gy", True)
    own1, own1_y, nz1 = own_x // 2, own_y // 2, nz // 2
    gathered = 2 * own1 * rows0 + 2 * own1 * own_y
    upward, downward, stack1, u0, *level0 = call(
        functools.partial(fine_first, size_x=size_x, size_y=size_y),
        [arr(4, own1 - 1, own1_y, nz1)] * 2 + [arr(4, own1, own1_y, nz1)]
        + [arr(own_x, own_y, nz)] + [arr(*window0)] * 7,
        [window0] * 3 + [(gathered, nz), (gathered, nz1)],
        *fields, xl, xr, yl, yr, cl, cr,
    )

    xl, xr = swap(upward, downward, "gx")
    (stack1,) = call(hand_on, [stack1], [], stack1)
    yl, yr = swap(stack1, stack1, "gy", True)
    (rim,) = call(join_rims, [arr(4, 2 * (own1 - 1), own1_y, nz1)], [], xl, xr, yl, yr)
    cl, cr = swap(rim, rim, "gy", True)
    planes1 = own1 + 2 * RIM_1
    window1 = (planes1, own1_y + 2 * RIM_1, nz1)
    sent_x = 2 * RIM_2 + 4 * RIM_X0
    sent_y = 8 + own_x
    upward, downward, y_upward, y_downward, stack2, *level1 = call(
        functools.partial(middle_first, size_x=size_x // 2, size_y=size_y // 2),
        [arr(sent_x, 8, LANES)] * 2 + [arr(sent_y, 8, LANES)] * 2 + [arr(2, 8, 8, LANES)] + [arr(*window1)] * 9,
        [window1] * 2 + [(16 * window1[1], 2 * nz1), (16 * window1[1], nz1)],
        stack1, xl, xr, yl, yr, cl, cr, u0,
    )

    xl, xr = swap(upward, downward, "gx")
    yl, yr = swap(y_upward, y_downward, "gy", True)
    rim = arr(4 * RIM_2 + 2 * RIM_X0, 8, LANES)
    cl, cr = swap(*call(pack_coarse, [rim, rim], [], xl, xr, yl, yr), "gy", True)
    planes2 = 2 * RIM_2 + 4
    window2 = (planes2, planes2, LANES)
    relaxed, part = call(
        functools.partial(coarse_and_last, size_x=size_x, size_y=size_y),
        [arr(own_x, own_y, nz), arr(8, LANES)],
        [window2] * 10 + [(LANES, LANES)] * 2 + [(8 * window1[1], LANES)]
        + [window1] * 2 + [(12 * 32, nz1)] + [window0] * 2 + [(12 * 32, nz)],
        xl, xr, yl, yr, cl, cr, stack2, u0, *level1, *level0,
    )
    total = sum_over(sum_over(part[:1], "gx"), "gy")[0, 0]
    return relaxed, jnp.sqrt(total / (size_x * size_y * nz))


def solution(mesh):
    specs = (P("gx", "gy", None),) * 4
    return jax.shard_map(
        body, mesh=mesh, in_specs=specs, out_specs=(P("gx", "gy", None), P()), check_vma=False
    )
```

```python
import functools

import jax
import jax.numpy as jnp
from jax import lax
from jax.experimental import pallas as pl
from jax.experimental.pallas import tpu as pltpu
from jax.sharding import PartitionSpec as P

OMEGA = 0.8
LN2 = 0.6931471805599453
F32 = jnp.float32
LANES = 128
VMEM_LIMIT = 24 * 1024 * 1024
AT_ONCE_0, AT_ONCE_1, AT_ONCE_2 = 1, 3, 7

RIM_X0, RIM_Y0 = 3, 4
RIM_1 = 8
RIM_2 = 6


def roll(value, shift, axis):
    return pltpu.roll(value, shift % value.shape[axis], axis)


def iota(shape, dim):
    return lax.broadcasted_iota(jnp.int32, shape, dim)


def shared_matrix(rows, cols, ratio_rows, ratio_cols, value):
    match = iota((rows, cols), 0) // ratio_rows == iota((rows, cols), 1) // ratio_cols
    return jnp.where(match, value, 0.0).astype(F32)


def dot(left, right):
    return jnp.dot(left, right, precision=lax.Precision.HIGHEST, preferred_element_type=F32)


def dot_parts(left, right):
    high = left.astype(jnp.bfloat16)
    rest = left - high.astype(F32)
    middle = rest.astype(jnp.bfloat16)
    low = (rest - middle.astype(F32)).astype(jnp.bfloat16)
    parts = jnp.concatenate([low, middle, high], axis=1)
    return jnp.dot(parts, jnp.concatenate([right.astype(jnp.bfloat16)] * 3, axis=0), preferred_element_type=F32)


def low_half(shape):
    return iota(shape, 0) < 4


def shifted_tiles(first, second, left, right):
    low = low_half(first.shape)
    a, b = roll(first, 4, 0), roll(second, 4, 0)
    return jnp.where(low, left, a), jnp.where(low, a, b), jnp.where(low, b, right)


def row_mask(shape, first_row, last_row, origin, size, lanes=None):
    row = iota(shape, 0)
    place = row + origin
    good = (row >= first_row) & (row < last_row) & (place >= 0) & (place < size)
    if lanes is not None:
        good = good & (iota(shape, 1) < lanes)
    return jnp.where(good, 1.0, 0.0).astype(F32)


def inner_sides(shape):
    place, last = lax.axis_index("gy"), lax.axis_size("gy") - 1
    row = iota(shape, 0)
    return row >= jnp.where(place == 0, shape[0], 0), row >= jnp.where(place == last, shape[0], 0)


def plane_bar(place, size):
    return jnp.where((place >= 0) & (place < size), 0.5, 2.0).astype(F32)


def over_planes(first, last, step):
    def loop_body(x, carry):
        step(x)
        return carry

    lax.fori_loop(first, last, loop_body, 0, unroll=last - first)


def fill_weights(e_ref, weights, planes, scale, wrap_free, first=0):
    wx, wy, wz, wb, total = weights
    half = 0.5 * scale
    shape = e_ref.shape[1:]
    lane = iota(shape, 1)
    last = shape[1] - 1

    def along_x(x):
        wx[x] = half * (e_ref[x] + e_ref[x + 1])

    over_planes(first, planes - 1 - first, along_x)

    def others(x):
        e = e_ref[x]
        y = half * (e + roll(e, -1, 0))
        z = half * (e + roll(e, -1, 1))
        if not wrap_free:
            z = jnp.where(lane < last, z, 0.0)
        faces = (wx[x] + wx[x - 1]) + (y + roll(y, 1, 0)) + (z + roll(z, 1, 1))
        if not wrap_free:
            b = jnp.where((lane == 0) | (lane == last), half * e, 0.0)
            wb[x] = b
            faces = faces + b
        wy[x] = y
        wz[x] = z
        total[x] = faces

    over_planes(first + 1, planes - 1 - first, others)


def planes_at(ref, x, count):
    if count == 1:
        return ref[x]
    return ref[x : x + count].reshape(count * ref.shape[1], ref.shape[2])


def runs(first, last, count):
    return [(x, min(count, last - x)) for x in range(first, last, count)]


def flux_of(x, u_ref, weights, count=1):
    wx, wy, wz, wb, _ = weights
    u = planes_at(u_ref, x, count)
    py = planes_at(wy, x, count) * (roll(u, -1, 0) - u)
    pz = planes_at(wz, x, count) * (roll(u, -1, 1) - u)
    flux = planes_at(wx, x - 1, count) * (u - planes_at(u_ref, x - 1, count))
    flux = flux - planes_at(wx, x, count) * (planes_at(u_ref, x + 1, count) - u)
    flux = flux + (roll(py, 1, 0) - py) + (roll(pz, 1, 1) - pz)
    if wb is not None:
        flux = flux + planes_at(wb, x, count) * u
    return u, flux


def halves(u):
    return jnp.exp(u - LN2), jnp.exp(-u - LN2)


def sweep(u_ref, out_ref, weights, k_ref, f_ref, first, last, rows, origin, size, at_once=1):
    height = u_ref.shape[1]
    for x, count in runs(first, last, at_once):
        u, flux = flux_of(x, u_ref, weights, count)
        up, down = halves(u)
        k = planes_at(k_ref, x, count)
        defect = planes_at(f_ref, x, count) - (flux + k * (up - down))
        slope = planes_at(weights[4], x, count) + k * (up + down)
        moved = u + OMEGA * defect / slope
        for i in range(count):
            plane = moved[i * height : (i + 1) * height]
            out_ref[x + i] = jnp.where(rows > plane_bar(origin + x + i, size), plane, 0.0)


def defect_at(x, u_ref, weights, k_ref, load, count=1):
    u, flux = flux_of(x, u_ref, weights, count)
    up, down = halves(u)
    return load - (flux + planes_at(k_ref, x, count) * (up - down))


def defects(u_ref, weights, k_ref, f_ref, first, last, at_once):
    height = u_ref.shape[1]
    for x, count in runs(first, last, at_once):
        d = defect_at(x, u_ref, weights, k_ref, planes_at(f_ref, x, count), count)
        for i in range(count):
            f_ref[x + i] = d[i * height : (i + 1) * height]


def pair_rows(ref, base, count=8):
    return ref[pl.ds(base, count, 2), :] + ref[pl.ds(base + 1, count, 2), :]


def rim_plane(x, brick, left, right, base, depth, rim):
    size = brick.shape[0]
    if x < rim:
        at = x - (rim - depth)
        return (left, base + at) if at >= 0 else None
    if x < rim + size:
        return (brick, x - rim)
    at = x - rim - size
    return (right, base + at) if at < depth else None


FINE_SENT = ((3, 0), (3, 3), (2, 6), (2, 8))


def fine_plane(x, index, brick, left, right):
    depth, base = FINE_SENT[index]
    return rim_plane(x, brick, left, right, base, depth, RIM_X0)


def tile_of(place, tile):
    if place is None:
        return None
    ref, x = place
    return ref[x, 8 * tile : 8 * tile + 8, :]


def pack_fine(bricks, planes, up_ref, down_ref):
    low = low_half(up_ref.shape[2:])
    for at, sources in enumerate(planes):
        for pair in range(2):
            first, second = (place(bricks) for place in sources[2 * pair : 2 * pair + 2])
            if first is None:
                up_ref[pair, at] = jnp.zeros(up_ref.shape[2:], F32)
                down_ref[pair, at] = jnp.zeros(up_ref.shape[2:], F32)
                continue
            up_ref[pair, at] = jnp.where(low, roll(tile_of(first, 1), 4, 0), tile_of(second, 1))
            down_ref[pair, at] = jnp.where(low, tile_of(first, 0), roll(tile_of(second, 0), 4, 0))


def pack_fine_own(s_ref, e_ref, k_ref, f_ref, up_ref, down_ref):
    planes = [
        [functools.partial(lambda refs, i, x: (refs[i], x), i=i, x=x) for i in range(4)]
        for x in range(s_ref.shape[0])
    ]
    pack_fine((s_ref, e_ref, k_ref, f_ref), planes, up_ref, down_ref)


def rim_planes(own):
    return list(range(RIM_X0)) + list(range(RIM_X0 + own, RIM_X0 + own + RIM_X0))


def pack_fine_rim(xl_ref, xr_ref, up_ref, down_ref):
    own = xl_ref.shape[1]
    brick = jax.ShapeDtypeStruct((own,), F32)
    planes = [
        [functools.partial(lambda refs, i, x: fine_plane(x, i, brick, *refs), i=i, x=x) for i in range(4)]
        for x in rim_planes(own)
    ]
    pack_fine((xl_ref, xr_ref), planes, up_ref, down_ref)


def join_rims(xl_ref, xr_ref, yl_ref, yr_ref, up_ref, down_ref):
    del yl_ref, yr_ref
    sent = xl_ref.shape[1] - 1
    for ref in (up_ref, down_ref):
        ref[:, :sent] = xl_ref[:, 1:]
        ref[:, sent:] = xr_ref[:, :sent]


def fine_first(
    s_ref, e_ref, k_ref, f_ref, xl_ref, xr_ref, yl_ref, yr_ref, cl_ref, cr_ref,
    up_ref, down_ref, y_up_ref, y_down_ref, stack_ref, u0_ref, kw_ref, fw_ref, wx, wy, wz, wb, total,
    ua, ub, ew_ref, gather, summed,
    *, size_x, size_y,
):
    bricks = (s_ref, e_ref, k_ref, f_ref)
    windows = (ua, ew_ref, kw_ref, fw_ref)
    own_x, own_y, nz = s_ref.shape
    planes = own_x + 2 * RIM_X0
    rows = own_y + 2 * RIM_Y0
    keep_left, keep_right = inner_sides((8, nz))
    corners = rim_planes(own_x)
    for x in range(planes):
        if x in corners:
            l_ref, r_ref, at = cl_ref, cr_ref, corners.index(x)
        else:
            l_ref, r_ref, at = yl_ref, yr_ref, x - RIM_X0
        for index in range(4):
            place = fine_plane(x, index, bricks[index], xl_ref, xr_ref)
            if place is None:
                windows[index][x] = jnp.zeros((rows, nz), F32)
                continue
            left = jnp.where(keep_left, l_ref[index // 2, at], 0.0)
            right = jnp.where(keep_right, r_ref[index // 2, at], 0.0)
            if index % 2 == 0:
                right = roll(right, 4, 0)
            else:
                left = roll(left, 4, 0)
            tiles = shifted_tiles(tile_of(place, 0), tile_of(place, 1), left, right)
            for i, tile in enumerate(tiles):
                windows[index][x, 8 * i : 8 * i + 8, :] = tile
    weights = (wx, wy, wz, wb, total)
    fill_weights(ew_ref, weights, planes, 1.0, False)
    origin_x = lax.axis_index("gx") * own_x - RIM_X0
    origin_y = lax.axis_index("gy") * own_y - RIM_Y0
    shape = (rows, nz)
    mask = row_mask(shape, 2, rows - 2, origin_y, size_y)
    sweep(ua, ub, weights, kw_ref, fw_ref, 1, planes - 1, mask, origin_x, size_x, AT_ONCE_0)
    mask = row_mask(shape, 3, rows - 3, origin_y, size_y)
    sweep(ub, ua, weights, kw_ref, fw_ref, 2, planes - 2, mask, origin_x, size_x, AT_ONCE_0)

    low = low_half((8, nz))
    pairs = own_x // 2

    def finish(j):
        x = RIM_X0 + 2 * j
        gather[pl.ds(j * rows, rows), :] = ua[x] + ua[x + 1]
        d = defect_at(x, ua, weights, kw_ref, fw_ref[x]) + defect_at(x + 1, ua, weights, kw_ref, fw_ref[x + 1])
        gather[pl.ds((pairs + j) * rows, rows), :] = d
        for i in range(2):
            u = ua[x + i]
            moved = [roll(u[8 * t : 8 * t + 8], 4, 0) for t in range(3)]
            u0_ref[2 * j + i, 0:8, :] = jnp.where(low, moved[0], moved[1])
            u0_ref[2 * j + i, 8:16, :] = jnp.where(low, moved[1], moved[2])

    over_planes(0, pairs, finish)
    base = 2 * pairs * rows
    for i, ref in enumerate((e_ref, k_ref)):
        for j in range(pairs):
            at = base + (i * pairs + j) * own_y
            gather[at : at + own_y, :] = ref[2 * j] + ref[2 * j + 1]
    summed[...] = dot(gather[...], shared_matrix(nz, nz // 2, 2, 1, 0.125))
    for j in range(pairs):
        tiles = (
            pair_rows(summed, base + j * own_y),
            pair_rows(summed, base + (pairs + j) * own_y),
            pair_rows(summed, j * rows + RIM_Y0),
            pair_rows(summed, (pairs + j) * rows + RIM_Y0),
        )
        for index, tile in enumerate(tiles):
            stack_ref[index, j] = tile
            y_up_ref[index, j] = tile
            y_down_ref[index, j] = tile
            up_ref[index, j] = tile
            down_ref[index, j] = tile


def middle_first(
    o_ref, xl_ref, xr_ref, yl_ref, yr_ref, cl_ref, cr_ref, u0_ref,
    up_ref, down_ref, y_up_ref, y_down_ref, stack_ref, w_ref, f_ref, k, v, wx, wy, wz, wb, total,
    e, wa, gather, summed,
    *, size_x, size_y,
):
    own, nz = o_ref.shape[2:]
    planes = own + 2 * RIM_1
    rows = own + 2 * RIM_1
    shape = (rows, nz)
    keep_left, keep_right = inner_sides((own, nz))
    sent = RIM_1 - 1

    def assemble(x, middle, left, right, at, side):
        for index, ref in enumerate((e, k, v, f_ref)):
            lower = jnp.where(keep_left, left[index, side], 0.0)
            upper = jnp.where(keep_right, right[index, side], 0.0)
            ref[x] = jnp.concatenate([lower, middle[index, at], upper], axis=0)

    for x in range(1, planes - 1):
        if x < RIM_1:
            assemble(x, xl_ref, cl_ref, cr_ref, x, x - 1)
        elif x < RIM_1 + own:
            assemble(x, o_ref, yl_ref, yr_ref, x - RIM_1, x - RIM_1)
        else:
            assemble(x, xr_ref, cl_ref, cr_ref, x - RIM_1 - own, sent + x - RIM_1 - own)
    weights = (wx, wy, wz, wb, total)
    fill_weights(e, weights, planes, 0.25, False, 1)
    origin_x = lax.axis_index("gx") * own - RIM_1
    origin_y = lax.axis_index("gy") * own - RIM_1

    defects(v, weights, k, f_ref, 2, planes - 2, AT_ONCE_1)
    mask = row_mask(shape, 2, rows - 2, origin_y, size_y)
    sweep(v, wa, weights, k, f_ref, 2, planes - 2, mask, origin_x, size_x, AT_ONCE_1)
    mask = row_mask(shape, 3, rows - 3, origin_y, size_y)
    sweep(wa, w_ref, weights, k, f_ref, 3, planes - 3, mask, origin_x, size_x, AT_ONCE_1)
    pairs = (planes - 8) // 2

    def finish(j):
        x = 4 + 2 * j
        d = defect_at(x, w_ref, weights, k, f_ref[x]) + defect_at(x + 1, w_ref, weights, k, f_ref[x + 1])
        at = pl.ds(j * rows, rows)
        gather[at, :nz] = e[x] + e[x + 1]
        gather[at, nz:] = k[x] + k[x + 1]
        at = pl.ds((pairs + j) * rows, rows)
        gather[at, :nz] = w_ref[x] + w_ref[x + 1]
        gather[at, nz:] = d

    over_planes(0, pairs, finish)
    summed[...] = dot(gather[...], shared_matrix(2 * nz, nz, 2, 1, 0.125))
    for a in range(2):
        for j in range(pairs):
            tile = pair_rows(summed, (a * pairs + j) * rows + 4)
            stack_ref[a, j] = tile
            if j < RIM_2:
                up_ref[a * RIM_2 + j] = tile
            if j >= pairs - RIM_2:
                down_ref[a * RIM_2 + j - (pairs - RIM_2)] = tile
    for a in range(2):
        for x in range(4):
            tile = stack_ref[a, pairs // 2 - 2 + x]
            y_up_ref[4 * a + x] = tile
            y_down_ref[4 * a + x] = tile
    own_planes = u0_ref.shape[0]
    for x in range(own_planes):
        tiles = quarter_tiles(u0_ref, x)
        y_up_ref[8 + x], y_down_ref[8 + x] = pack_rows(tiles)
        for t in range(4):
            if x < RIM_X0:
                down_ref[2 * RIM_2 + 4 * x + t] = tiles[t]
            if x >= own_planes - RIM_X0:
                up_ref[2 * RIM_2 + 4 * (x - own_planes + RIM_X0) + t] = tiles[t]


def quarter_tiles(ref, x):
    return [ref[x, 8 * (t // 2) : 8 * (t // 2) + 8, LANES * (t % 2) : LANES * (t % 2) + LANES] for t in range(4)]


def pack_rows(tiles):
    low = low_half(tiles[0].shape)
    last = jnp.where(low, roll(tiles[2], 4, 0), tiles[3])
    return last, jnp.where(low, tiles[0], roll(tiles[1], 4, 0))


def pack_coarse(xl_ref, xr_ref, yl_ref, yr_ref, up_ref, down_ref):
    del yl_ref, yr_ref
    for a in range(2):
        for x in range(2 * RIM_2):
            tile = xl_ref[a * RIM_2 + x] if x < RIM_2 else xr_ref[a * RIM_2 + x - RIM_2]
            up_ref[2 * RIM_2 * a + x] = tile
            down_ref[2 * RIM_2 * a + x] = tile
    for x in range(2 * RIM_X0):
        ref, at = (xl_ref, x) if x < RIM_X0 else (xr_ref, x - RIM_X0)
        tiles = [ref[2 * RIM_2 + 4 * at + t] for t in range(4)]
        up_ref[4 * RIM_2 + x], down_ref[4 * RIM_2 + x] = pack_rows(tiles)


def coarse_and_last(
    xl_ref, xr_ref, yl_ref, yr_ref, cl_ref, cr_ref, o2_ref, u0_ref,
    w1_ref, f1_ref, k1, v1_ref, wx1, wy1, wz1, wb1, t1,
    kw_ref, fw_ref, wx0, wy0, wz0, wb0, t0,
    out_ref, part_ref,
    e2, k2, v2, f2, a2, b2, wx2, wy2, wz2, t2, q2, s2, d2,
    a1, b1, d1, a0, b0, q0,
    *, size_x, size_y,
):
    place_x, place_y = lax.axis_index("gx"), lax.axis_index("gy")
    planes2 = 2 * RIM_2 + 4
    rows2 = planes2
    shape2 = (rows2, LANES)
    nz2 = LANES // 2
    row8 = iota((8, LANES), 0)
    inside = iota(shape2, 1) < nz2
    keep_left, keep_right = inner_sides((8, LANES))

    spare = o2_ref.shape[1] // 2 - 2

    def window2(a, x):
        if x < RIM_2:
            own, at = xl_ref[a * RIM_2 + x], 2 * RIM_2 * a + x
            left, right = cl_ref[at], cr_ref[at]
        elif x < RIM_2 + 4:
            own, at = o2_ref[a, spare + x - RIM_2], 4 * a + x - RIM_2
            left, right = yl_ref[at], yr_ref[at]
        else:
            own, at = xr_ref[a * RIM_2 + x - RIM_2 - 4], 2 * RIM_2 * a + x - 4
            left, right = cl_ref[at], cr_ref[at]
        own = roll(own, 4, 0)
        upper = jnp.where(row8 >= 6, own, jnp.where(keep_left, left, 0.0))
        lower = jnp.where(row8 < 2, own, jnp.where(keep_right, right, 0.0))
        return jnp.concatenate([upper, lower], axis=0)

    for x in range(planes2):
        both = window2(0, x)
        e2[x] = jnp.where(inside, both, 0.0)
        k2[x] = jnp.where(inside, roll(both, nz2, 1), 0.0)
        both = window2(1, x)
        v2[x] = jnp.where(inside, both, 0.0)
        f2[x] = jnp.where(inside, roll(both, nz2, 1), 0.0)

    weights2 = (wx2, wy2, wz2, None, t2)
    fill_weights(e2, weights2, planes2, 0.0625, True)
    origin_x = place_x * 4 - RIM_2
    origin_y = place_y * 4 - RIM_2

    defects(v2, weights2, k2, f2, 1, planes2 - 1, AT_ONCE_2)
    source = v2
    for i in range(4):
        target = a2 if i % 2 == 0 else b2
        mask = row_mask(shape2, 1 + i, rows2 - 1 - i, origin_y, size_y // 4, nz2)
        last = planes2 - 1 - i
        sweep(source, target, weights2, k2, f2, 1 + i, last, mask, origin_x, size_x // 4, AT_ONCE_2)
        source = target
    for j in range(8):
        q2[16 * j : 16 * j + 16, :] = source[4 + j] - v2[4 + j]
    s2[...] = dot_parts(q2[...], shared_matrix(LANES, LANES, 1, 2, 1.0))
    planes1, rows1, nz1 = w1_ref.shape
    d2[...] = jnp.zeros(d2.shape, F32)
    for j in range(8):
        rows = roll(s2[16 * j : 16 * j + 16, :], -4, 0)[:8]
        d2[pl.ds(rows1 * j + 4, 8, 2), :] = rows
        d2[pl.ds(rows1 * j + 5, 8, 2), :] = rows

    own1 = planes1 - 2 * RIM_1
    shape1 = (rows1, nz1)
    weights1 = (wx1, wy1, wz1, wb1, t1)
    origin_x = place_x * own1 - RIM_1
    origin_y = place_y * own1 - RIM_1
    for x in range(4, 20):
        at = rows1 * ((x - 4) // 2)
        a1[x] = w1_ref[x] + d2[at : at + rows1, :]
    mask = row_mask(shape1, 5, rows1 - 5, origin_y, size_y // 2)
    sweep(a1, b1, weights1, k1, f1_ref, 5, planes1 - 5, mask, origin_x, size_x // 2, AT_ONCE_1)
    mask = row_mask(shape1, 6, rows1 - 6, origin_y, size_y // 2)
    sweep(b1, a1, weights1, k1, f1_ref, 6, planes1 - 6, mask, origin_x, size_x // 2, AT_ONCE_1)
    for j in range(12):
        rows = roll(a1[6 + j] - v1_ref[6 + j], -6, 0)[:16]
        d1[pl.ds(32 * j, 16, 2), :] = rows
        d1[pl.ds(32 * j + 1, 16, 2), :] = rows
    nz0 = 2 * nz1
    q0[...] = dot_parts(d1[...], shared_matrix(nz1, nz0, 1, 2, 1.0))

    own_x, own_y = out_ref.shape[:2]
    planes0 = own_x + 2 * RIM_X0
    rows0 = own_y + 2 * RIM_Y0
    shape0 = (rows0, nz0)
    corners = rim_planes(own_x)
    for x in range(planes0):
        if x in corners:
            at = corners.index(x)
            ref, first = (xl_ref, at) if x < RIM_X0 else (xr_ref, at - RIM_X0)
            tiles = [ref[2 * RIM_2 + 4 * first + t] for t in range(4)]
            left, right = cl_ref[4 * RIM_2 + at], cr_ref[4 * RIM_2 + at]
        else:
            tiles = quarter_tiles(u0_ref, x - RIM_X0)
            left, right = yl_ref[8 + x - RIM_X0], yr_ref[8 + x - RIM_X0]
        upper = jnp.concatenate(tiles[:2], axis=1)
        lower = jnp.concatenate(tiles[2:], axis=1)
        left = jnp.where(keep_left, left, 0.0)
        right = jnp.where(keep_right, right, 0.0)
        left = jnp.concatenate([left, roll(left, 4, 0)], axis=1)
        right = jnp.concatenate([roll(right, 4, 0), right], axis=1)
        tiles = shifted_tiles(upper, lower, left, right)
        at = 32 * ((x + 1) // 2)
        for i, tile in enumerate(tiles):
            a0[x, 8 * i : 8 * i + 8, :] = tile + q0[at + 8 * i : at + 8 * i + 8, :]
    weights0 = (wx0, wy0, wz0, wb0, t0)
    origin_x = place_x * own_x - RIM_X0
    origin_y = place_y * own_y - RIM_Y0
    mask = row_mask(shape0, 2, rows0 - 2, origin_y, size_y)
    sweep(a0, b0, weights0, kw_ref, fw_ref, 1, planes0 - 1, mask, origin_x, size_x, AT_ONCE_0)
    mask = row_mask(shape0, 3, rows0 - 3, origin_y, size_y)
    sweep(b0, a0, weights0, kw_ref, fw_ref, 2, planes0 - 2, mask, origin_x, size_x, AT_ONCE_0)
    low = low_half((8, nz0))

    def finish(x, acc):
        d = defect_at(x, a0, weights0, kw_ref, fw_ref[x])
        u = a0[x]
        moved = [roll(u[8 * t : 8 * t + 8], 4, 0) for t in range(3)]
        out_ref[x - RIM_X0, 0:8, :] = jnp.where(low, moved[0], moved[1])
        out_ref[x - RIM_X0, 8:16, :] = jnp.where(low, moved[1], moved[2])
        return acc + d * d

    acc = lax.fori_loop(RIM_X0, RIM_X0 + own_x, finish, jnp.zeros(shape0, F32), unroll=own_x)
    row = iota(shape0, 0)
    acc = jnp.where((row >= RIM_Y0) & (row < RIM_Y0 + own_y), acc, 0.0)
    acc = jnp.sum(acc, axis=0, keepdims=True)
    acc = jnp.sum(acc, axis=1, keepdims=True)
    part_ref[...] = jnp.broadcast_to(acc, part_ref.shape)


def arr(*shape):
    return jax.ShapeDtypeStruct(shape, F32)


def call(kernel, outs, scratch, *args):
    return pl.pallas_call(
        kernel,
        out_shape=outs,
        in_specs=[pl.BlockSpec(memory_space=pltpu.VMEM)] * len(args),
        out_specs=[pl.BlockSpec(memory_space=pltpu.VMEM)] * len(outs),
        scratch_shapes=[pltpu.VMEM(shape, F32) for shape in scratch],
        compiler_params=pltpu.CompilerParams(vmem_limit_bytes=VMEM_LIMIT),
    )(*args)


def swap(upward, downward, axis, ring=False):
    size = lax.axis_size(axis)
    up = [(i, (i + 1) % size) for i in range(size if ring else size - 1)]
    down = [(j, i) for i, j in up]
    return lax.ppermute(upward, axis, up), lax.ppermute(downward, axis, down)


def sum_over(part, axis):
    size = lax.axis_size(axis)
    rows = jnp.broadcast_to(part, (size, LANES))
    return jnp.sum(lax.all_to_all(rows, axis, 0, 0, tiled=True), axis=0, keepdims=True)


def body(start, permit, ion, source):
    own_x, own_y, nz = start.shape
    size_x, size_y = own_x * lax.axis_size("gx"), own_y * lax.axis_size("gy")
    planes0, rows0 = own_x + 2 * RIM_X0, own_y + 2 * RIM_Y0
    window0 = (planes0, rows0, nz)

    fields = (start, permit, ion, source)
    depths = [depth for depth, _ in FINE_SENT]
    upward = jnp.concatenate([a[own_x - d :] for a, d in zip(fields, depths)], axis=0)
    downward = jnp.concatenate([a[:d] for a, d in zip(fields, depths)], axis=0)
    xl, xr = swap(upward, downward, "gx")
    yl, yr = swap(*call(pack_fine_own, [arr(2, own_x, 8, nz)] * 2, [], *fields), "gy", True)
    cl, cr = swap(*call(pack_fine_rim, [arr(2, 2 * RIM_X0, 8, nz)] * 2, [], xl, xr), "gy", True)
    own1, own1_y, nz1 = own_x // 2, own_y // 2, nz // 2
    gathered = 2 * own1 * rows0 + 2 * own1 * own_y
    upward, downward, y_upward, y_downward, stack1, u0, *level0 = call(
        functools.partial(fine_first, size_x=size_x, size_y=size_y),
        [arr(4, own1, own1_y, nz1)] * 5
        + [arr(own_x, own_y, nz)] + [arr(*window0)] * 7,
        [window0] * 3 + [(gathered, nz), (gathered, nz1)],
        *fields, xl, xr, yl, yr, cl, cr,
    )

    xl, xr = swap(upward, downward, "gx")
    yl, yr = swap(y_upward, y_downward, "gy", True)
    rim = arr(4, 2 * (own1 - 1), own1_y, nz1)
    cl, cr = swap(*call(join_rims, [rim, rim], [], xl, xr, yl, yr), "gy", True)
    planes1 = own1 + 2 * RIM_1
    window1 = (planes1, own1_y + 2 * RIM_1, nz1)
    sent_x = 2 * RIM_2 + 4 * RIM_X0
    sent_y = 8 + own_x
    upward, downward, y_upward, y_downward, stack2, *level1 = call(
        functools.partial(middle_first, size_x=size_x // 2, size_y=size_y // 2),
        [arr(sent_x, 8, LANES)] * 2 + [arr(sent_y, 8, LANES)] * 2 + [arr(2, 8, 8, LANES)] + [arr(*window1)] * 9,
        [window1] * 2 + [(16 * window1[1], 2 * nz1), (16 * window1[1], nz1)],
        stack1, xl, xr, yl, yr, cl, cr, u0,
    )

    xl, xr = swap(upward, downward, "gx")
    yl, yr = swap(y_upward, y_downward, "gy", True)
    rim = arr(4 * RIM_2 + 2 * RIM_X0, 8, LANES)
    cl, cr = swap(*call(pack_coarse, [rim, rim], [], xl, xr, yl, yr), "gy", True)
    planes2 = 2 * RIM_2 + 4
    window2 = (planes2, planes2, LANES)
    relaxed, part = call(
        functools.partial(coarse_and_last, size_x=size_x, size_y=size_y),
        [arr(own_x, own_y, nz), arr(8, LANES)],
        [window2] * 10 + [(LANES, LANES)] * 2 + [(8 * window1[1], LANES)]
        + [window1] * 2 + [(12 * 32, nz1)] + [window0] * 2 + [(12 * 32, nz)],
        xl, xr, yl, yr, cl, cr, stack2, u0, *level1, *level0,
    )
    total = sum_over(sum_over(part[:1], "gx"), "gy")[0, 0]
    return relaxed, jnp.sqrt(total / (size_x * size_y * nz))


def solution(mesh):
    specs = (P("gx", "gy", None),) * 4
    return jax.shard_map(
        body, mesh=mesh, in_specs=specs, out_specs=(P("gx", "gy", None), P()), check_vma=False
    )
```

```python
import functools

import jax
import jax.numpy as jnp
from jax import lax
from jax.experimental import pallas as pl
from jax.experimental.pallas import tpu as pltpu
from jax.sharding import PartitionSpec as P

OMEGA = 0.8
LN2 = 0.6931471805599453
F32 = jnp.float32
LANES = 128
VMEM_LIMIT = 24 * 1024 * 1024
AT_ONCE_0, AT_ONCE_1, AT_ONCE_2 = 1, 3, 14

RIM_X0, RIM_Y0 = 3, 4
RIM_1 = 8
RIM_2 = 6


def roll(value, shift, axis):
    return pltpu.roll(value, shift % value.shape[axis], axis)


def iota(shape, dim):
    return lax.broadcasted_iota(jnp.int32, shape, dim)


def shared_matrix(rows, cols, ratio_rows, ratio_cols, value):
    match = iota((rows, cols), 0) // ratio_rows == iota((rows, cols), 1) // ratio_cols
    return jnp.where(match, value, 0.0).astype(F32)


def dot(left, right):
    return jnp.dot(left, right, precision=lax.Precision.HIGHEST, preferred_element_type=F32)


def dot_parts(left, right):
    high = left.astype(jnp.bfloat16)
    rest = left - high.astype(F32)
    middle = rest.astype(jnp.bfloat16)
    low = (rest - middle.astype(F32)).astype(jnp.bfloat16)
    parts = jnp.concatenate([low, middle, high], axis=1)
    return jnp.dot(parts, jnp.concatenate([right.astype(jnp.bfloat16)] * 3, axis=0), preferred_element_type=F32)


def low_half(shape):
    return iota(shape, 0) < 4


def shifted_tiles(first, second, left, right):
    low = low_half(first.shape)
    a, b = roll(first, 4, 0), roll(second, 4, 0)
    return jnp.where(low, left, a), jnp.where(low, a, b), jnp.where(low, b, right)


def row_mask(shape, first_row, last_row, origin, size, lanes=None):
    row = iota(shape, 0)
    place = row + origin
    good = (row >= first_row) & (row < last_row) & (place >= 0) & (place < size)
    if lanes is not None:
        good = good & (iota(shape, 1) < lanes)
    return jnp.where(good, 1.0, 0.0).astype(F32)


def inner_sides(shape):
    place, last = lax.axis_index("gy"), lax.axis_size("gy") - 1
    row = iota(shape, 0)
    return row >= jnp.where(place == 0, shape[0], 0), row >= jnp.where(place == last, shape[0], 0)


def plane_bar(place, size):
    return jnp.where((place >= 0) & (place < size), 0.5, 2.0).astype(F32)


def over_planes(first, last, step):
    def loop_body(x, carry):
        step(x)
        return carry

    lax.fori_loop(first, last, loop_body, 0, unroll=last - first)


def fill_weights(e_ref, weights, planes, scale, wrap_free, first=0):
    wx, wy, wz, wb, total = weights
    half = 0.5 * scale
    shape = e_ref.shape[1:]
    lane = iota(shape, 1)
    last = shape[1] - 1

    def along_x(x):
        wx[x] = half * (e_ref[x] + e_ref[x + 1])

    over_planes(first, planes - 1 - first, along_x)

    def others(x):
        e = e_ref[x]
        y = half * (e + roll(e, -1, 0))
        z = half * (e + roll(e, -1, 1))
        if not wrap_free:
            z = jnp.where(lane < last, z, 0.0)
        faces = (wx[x] + wx[x - 1]) + (y + roll(y, 1, 0)) + (z + roll(z, 1, 1))
        if not wrap_free:
            b = jnp.where((lane == 0) | (lane == last), half * e, 0.0)
            wb[x] = b
            faces = faces + b
        wy[x] = y
        wz[x] = z
        total[x] = faces

    over_planes(first + 1, planes - 1 - first, others)


def planes_at(ref, x, count):
    if count == 1:
        return ref[x]
    return ref[x : x + count].reshape(count * ref.shape[1], ref.shape[2])


def runs(first, last, count):
    return [(x, min(count, last - x)) for x in range(first, last, count)]


def flux_of(x, u_ref, weights, count=1):
    wx, wy, wz, wb, _ = weights
    u = planes_at(u_ref, x, count)
    py = planes_at(wy, x, count) * (roll(u, -1, 0) - u)
    pz = planes_at(wz, x, count) * (roll(u, -1, 1) - u)
    flux = planes_at(wx, x - 1, count) * (u - planes_at(u_ref, x - 1, count))
    flux = flux - planes_at(wx, x, count) * (planes_at(u_ref, x + 1, count) - u)
    flux = flux + (roll(py, 1, 0) - py) + (roll(pz, 1, 1) - pz)
    if wb is not None:
        flux = flux + planes_at(wb, x, count) * u
    return u, flux


def halves(u):
    return jnp.exp(u - LN2), jnp.exp(-u - LN2)


def sweep(u_ref, out_ref, weights, k_ref, f_ref, first, last, rows, origin, size, at_once=1):
    height = u_ref.shape[1]
    for x, count in runs(first, last, at_once):
        u, flux = flux_of(x, u_ref, weights, count)
        up, down = halves(u)
        k = planes_at(k_ref, x, count)
        defect = planes_at(f_ref, x, count) - (flux + k * (up - down))
        slope = planes_at(weights[4], x, count) + k * (up + down)
        moved = u + OMEGA * defect / slope
        for i in range(count):
            plane = moved[i * height : (i + 1) * height]
            out_ref[x + i] = jnp.where(rows > plane_bar(origin + x + i, size), plane, 0.0)


def defect_at(x, u_ref, weights, k_ref, load, count=1):
    u, flux = flux_of(x, u_ref, weights, count)
    up, down = halves(u)
    return load - (flux + planes_at(k_ref, x, count) * (up - down))


def defects(u_ref, weights, k_ref, f_ref, first, last, at_once):
    height = u_ref.shape[1]
    for x, count in runs(first, last, at_once):
        d = defect_at(x, u_ref, weights, k_ref, planes_at(f_ref, x, count), count)
        for i in range(count):
            f_ref[x + i] = d[i * height : (i + 1) * height]


def pair_rows(ref, base, count=8):
    return ref[pl.ds(base, count, 2), :] + ref[pl.ds(base + 1, count, 2), :]


def rim_plane(x, brick, left, right, base, depth, rim):
    size = brick.shape[0]
    if x < rim:
        at = x - (rim - depth)
        return (left, base + at) if at >= 0 else None
    if x < rim + size:
        return (brick, x - rim)
    at = x - rim - size
    return (right, base + at) if at < depth else None


FINE_SENT = ((3, 0), (3, 3), (2, 6), (2, 8))


def fine_plane(x, index, brick, left, right):
    depth, base = FINE_SENT[index]
    return rim_plane(x, brick, left, right, base, depth, RIM_X0)


def tile_of(place, tile):
    if place is None:
        return None
    ref, x = place
    return ref[x, 8 * tile : 8 * tile + 8, :]


def pack_fine(bricks, planes, up_ref, down_ref):
    low = low_half(up_ref.shape[2:])
    for at, sources in enumerate(planes):
        for pair in range(2):
            first, second = (place(bricks) for place in sources[2 * pair : 2 * pair + 2])
            if first is None:
                up_ref[pair, at] = jnp.zeros(up_ref.shape[2:], F32)
                down_ref[pair, at] = jnp.zeros(up_ref.shape[2:], F32)
                continue
            up_ref[pair, at] = jnp.where(low, roll(tile_of(first, 1), 4, 0), tile_of(second, 1))
            down_ref[pair, at] = jnp.where(low, tile_of(first, 0), roll(tile_of(second, 0), 4, 0))


def pack_fine_own(s_ref, e_ref, k_ref, f_ref, up_ref, down_ref):
    planes = [
        [functools.partial(lambda refs, i, x: (refs[i], x), i=i, x=x) for i in range(4)]
        for x in range(s_ref.shape[0])
    ]
    pack_fine((s_ref, e_ref, k_ref, f_ref), planes, up_ref, down_ref)


def rim_planes(own):
    return list(range(RIM_X0)) + list(range(RIM_X0 + own, RIM_X0 + own + RIM_X0))


def pack_fine_rim(xl_ref, xr_ref, up_ref, down_ref):
    own = xl_ref.shape[1]
    brick = jax.ShapeDtypeStruct((own,), F32)
    planes = [
        [functools.partial(lambda refs, i, x: fine_plane(x, i, brick, *refs), i=i, x=x) for i in range(4)]
        for x in rim_planes(own)
    ]
    pack_fine((xl_ref, xr_ref), planes, up_ref, down_ref)


def join_rims(xl_ref, xr_ref, yl_ref, yr_ref, up_ref, down_ref):
    del yl_ref, yr_ref
    sent = xl_ref.shape[1] - 1
    for ref in (up_ref, down_ref):
        ref[:, :sent] = xl_ref[:, 1:]
        ref[:, sent:] = xr_ref[:, :sent]


def fine_first(
    s_ref, e_ref, k_ref, f_ref, xl_ref, xr_ref, yl_ref, yr_ref, cl_ref, cr_ref,
    up_ref, down_ref, y_up_ref, y_down_ref, stack_ref, u0_ref, kw_ref, fw_ref, wx, wy, wz, wb, total,
    ua, ub, ew_ref, gather, summed,
    *, size_x, size_y,
):
    bricks = (s_ref, e_ref, k_ref, f_ref)
    windows = (ua, ew_ref, kw_ref, fw_ref)
    own_x, own_y, nz = s_ref.shape
    planes = own_x + 2 * RIM_X0
    rows = own_y + 2 * RIM_Y0
    keep_left, keep_right = inner_sides((8, nz))
    corners = rim_planes(own_x)
    for x in range(planes):
        if x in corners:
            l_ref, r_ref, at = cl_ref, cr_ref, corners.index(x)
        else:
            l_ref, r_ref, at = yl_ref, yr_ref, x - RIM_X0
        for index in range(4):
            place = fine_plane(x, index, bricks[index], xl_ref, xr_ref)
            if place is None:
                windows[index][x] = jnp.zeros((rows, nz), F32)
                continue
            left = jnp.where(keep_left, l_ref[index // 2, at], 0.0)
            right = jnp.where(keep_right, r_ref[index // 2, at], 0.0)
            if index % 2 == 0:
                right = roll(right, 4, 0)
            else:
                left = roll(left, 4, 0)
            tiles = shifted_tiles(tile_of(place, 0), tile_of(place, 1), left, right)
            for i, tile in enumerate(tiles):
                windows[index][x, 8 * i : 8 * i + 8, :] = tile
    weights = (wx, wy, wz, wb, total)
    fill_weights(ew_ref, weights, planes, 1.0, False)
    origin_x = lax.axis_index("gx") * own_x - RIM_X0
    origin_y = lax.axis_index("gy") * own_y - RIM_Y0
    shape = (rows, nz)
    mask = row_mask(shape, 2, rows - 2, origin_y, size_y)
    sweep(ua, ub, weights, kw_ref, fw_ref, 1, planes - 1, mask, origin_x, size_x, AT_ONCE_0)
    mask = row_mask(shape, 3, rows - 3, origin_y, size_y)
    sweep(ub, ua, weights, kw_ref, fw_ref, 2, planes - 2, mask, origin_x, size_x, AT_ONCE_0)

    low = low_half((8, nz))
    pairs = own_x // 2

    def finish(j):
        x = RIM_X0 + 2 * j
        gather[pl.ds(j * rows, rows), :] = ua[x] + ua[x + 1]
        d = defect_at(x, ua, weights, kw_ref, fw_ref[x]) + defect_at(x + 1, ua, weights, kw_ref, fw_ref[x + 1])
        gather[pl.ds((pairs + j) * rows, rows), :] = d
        for i in range(2):
            u = ua[x + i]
            moved = [roll(u[8 * t : 8 * t + 8], 4, 0) for t in range(3)]
            u0_ref[2 * j + i, 0:8, :] = jnp.where(low, moved[0], moved[1])
            u0_ref[2 * j + i, 8:16, :] = jnp.where(low, moved[1], moved[2])

    over_planes(0, pairs, finish)
    base = 2 * pairs * rows
    for i, ref in enumerate((e_ref, k_ref)):
        for j in range(pairs):
            at = base + (i * pairs + j) * own_y
            gather[at : at + own_y, :] = ref[2 * j] + ref[2 * j + 1]
    summed[...] = dot(gather[...], shared_matrix(nz, nz // 2, 2, 1, 0.125))
    for j in range(pairs):
        tiles = (
            pair_rows(summed, base + j * own_y),
            pair_rows(summed, base + (pairs + j) * own_y),
            pair_rows(summed, j * rows + RIM_Y0),
            pair_rows(summed, (pairs + j) * rows + RIM_Y0),
        )
        for index, tile in enumerate(tiles):
            stack_ref[index, j] = tile
            y_up_ref[index, j] = tile
            y_down_ref[index, j] = tile
            up_ref[index, j] = tile
            down_ref[index, j] = tile


def middle_first(
    o_ref, xl_ref, xr_ref, yl_ref, yr_ref, cl_ref, cr_ref, u0_ref,
    up_ref, down_ref, y_up_ref, y_down_ref, stack_ref, w_ref, f_ref, k, v, wx, wy, wz, wb, total,
    e, wa, gather, summed,
    *, size_x, size_y,
):
    own, nz = o_ref.shape[2:]
    planes = own + 2 * RIM_1
    rows = own + 2 * RIM_1
    shape = (rows, nz)
    keep_left, keep_right = inner_sides((own, nz))
    sent = RIM_1 - 1

    def assemble(x, middle, left, right, at, side):
        for index, ref in enumerate((e, k, v, f_ref)):
            lower = jnp.where(keep_left, left[index, side], 0.0)
            upper = jnp.where(keep_right, right[index, side], 0.0)
            ref[x] = jnp.concatenate([lower, middle[index, at], upper], axis=0)

    for x in range(1, planes - 1):
        if x < RIM_1:
            assemble(x, xl_ref, cl_ref, cr_ref, x, x - 1)
        elif x < RIM_1 + own:
            assemble(x, o_ref, yl_ref, yr_ref, x - RIM_1, x - RIM_1)
        else:
            assemble(x, xr_ref, cl_ref, cr_ref, x - RIM_1 - own, sent + x - RIM_1 - own)
    weights = (wx, wy, wz, wb, total)
    fill_weights(e, weights, planes, 0.25, False, 1)
    origin_x = lax.axis_index("gx") * own - RIM_1
    origin_y = lax.axis_index("gy") * own - RIM_1

    defects(v, weights, k, f_ref, 2, planes - 2, AT_ONCE_1)
    mask = row_mask(shape, 2, rows - 2, origin_y, size_y)
    sweep(v, wa, weights, k, f_ref, 2, planes - 2, mask, origin_x, size_x, AT_ONCE_1)
    mask = row_mask(shape, 3, rows - 3, origin_y, size_y)
    sweep(wa, w_ref, weights, k, f_ref, 3, planes - 3, mask, origin_x, size_x, AT_ONCE_1)
    pairs = (planes - 8) // 2

    def finish(j):
        x = 4 + 2 * j
        d = defect_at(x, w_ref, weights, k, f_ref[x]) + defect_at(x + 1, w_ref, weights, k, f_ref[x + 1])
        at = pl.ds(j * rows, rows)
        gather[at, :nz] = e[x] + e[x + 1]
        gather[at, nz:] = k[x] + k[x + 1]
        at = pl.ds((pairs + j) * rows, rows)
        gather[at, :nz] = w_ref[x] + w_ref[x + 1]
        gather[at, nz:] = d

    over_planes(0, pairs, finish)
    summed[...] = dot(gather[...], shared_matrix(2 * nz, nz, 2, 1, 0.125))
    for a in range(2):
        for j in range(pairs):
            tile = pair_rows(summed, (a * pairs + j) * rows + 4)
            stack_ref[a, j] = tile
            if j < RIM_2:
                up_ref[a * RIM_2 + j] = tile
            if j >= pairs - RIM_2:
                down_ref[a * RIM_2 + j - (pairs - RIM_2)] = tile
    for a in range(2):
        for x in range(4):
            tile = stack_ref[a, pairs // 2 - 2 + x]
            y_up_ref[4 * a + x] = tile
            y_down_ref[4 * a + x] = tile
    own_planes = u0_ref.shape[0]
    for x in range(own_planes):
        tiles = quarter_tiles(u0_ref, x)
        y_up_ref[8 + x], y_down_ref[8 + x] = pack_rows(tiles)
        for t in range(4):
            if x < RIM_X0:
                down_ref[2 * RIM_2 + 4 * x + t] = tiles[t]
            if x >= own_planes - RIM_X0:
                up_ref[2 * RIM_2 + 4 * (x - own_planes + RIM_X0) + t] = tiles[t]


def quarter_tiles(ref, x):
    return [ref[x, 8 * (t // 2) : 8 * (t // 2) + 8, LANES * (t % 2) : LANES * (t % 2) + LANES] for t in range(4)]


def pack_rows(tiles):
    low = low_half(tiles[0].shape)
    last = jnp.where(low, roll(tiles[2], 4, 0), tiles[3])
    return last, jnp.where(low, tiles[0], roll(tiles[1], 4, 0))


def pack_coarse(xl_ref, xr_ref, yl_ref, yr_ref, up_ref, down_ref):
    del yl_ref, yr_ref
    for a in range(2):
        for x in range(2 * RIM_2):
            tile = xl_ref[a * RIM_2 + x] if x < RIM_2 else xr_ref[a * RIM_2 + x - RIM_2]
            up_ref[2 * RIM_2 * a + x] = tile
            down_ref[2 * RIM_2 * a + x] = tile
    for x in range(2 * RIM_X0):
        ref, at = (xl_ref, x) if x < RIM_X0 else (xr_ref, x - RIM_X0)
        tiles = [ref[2 * RIM_2 + 4 * at + t] for t in range(4)]
        up_ref[4 * RIM_2 + x], down_ref[4 * RIM_2 + x] = pack_rows(tiles)


def coarse_and_last(
    xl_ref, xr_ref, yl_ref, yr_ref, cl_ref, cr_ref, o2_ref, u0_ref,
    w1_ref, f1_ref, k1, v1_ref, wx1, wy1, wz1, wb1, t1,
    kw_ref, fw_ref, wx0, wy0, wz0, wb0, t0,
    out_ref, part_ref,
    e2, k2, v2, f2, a2, b2, wx2, wy2, wz2, t2, q2, s2, d2,
    a1, b1, d1, a0, b0, q0,
    *, size_x, size_y,
):
    place_x, place_y = lax.axis_index("gx"), lax.axis_index("gy")
    planes2 = 2 * RIM_2 + 4
    rows2 = planes2
    shape2 = (rows2, LANES)
    nz2 = LANES // 2
    row8 = iota((8, LANES), 0)
    inside = iota(shape2, 1) < nz2
    keep_left, keep_right = inner_sides((8, LANES))

    spare = o2_ref.shape[1] // 2 - 2

    def window2(a, x):
        if x < RIM_2:
            own, at = xl_ref[a * RIM_2 + x], 2 * RIM_2 * a + x
            left, right = cl_ref[at], cr_ref[at]
        elif x < RIM_2 + 4:
            own, at = o2_ref[a, spare + x - RIM_2], 4 * a + x - RIM_2
            left, right = yl_ref[at], yr_ref[at]
        else:
            own, at = xr_ref[a * RIM_2 + x - RIM_2 - 4], 2 * RIM_2 * a + x - 4
            left, right = cl_ref[at], cr_ref[at]
        own = roll(own, 4, 0)
        upper = jnp.where(row8 >= 6, own, jnp.where(keep_left, left, 0.0))
        lower = jnp.where(row8 < 2, own, jnp.where(keep_right, right, 0.0))
        return jnp.concatenate([upper, lower], axis=0)

    for x in range(planes2):
        both = window2(0, x)
        e2[x] = jnp.where(inside, both, 0.0)
        k2[x] = jnp.where(inside, roll(both, nz2, 1), 0.0)
        both = window2(1, x)
        v2[x] = jnp.where(inside, both, 0.0)
        f2[x] = jnp.where(inside, roll(both, nz2, 1), 0.0)

    weights2 = (wx2, wy2, wz2, None, t2)
    fill_weights(e2, weights2, planes2, 0.0625, True)
    origin_x = place_x * 4 - RIM_2
    origin_y = place_y * 4 - RIM_2

    defects(v2, weights2, k2, f2, 1, planes2 - 1, AT_ONCE_2)
    source = v2
    for i in range(4):
        target = a2 if i % 2 == 0 else b2
        mask = row_mask(shape2, 1 + i, rows2 - 1 - i, origin_y, size_y // 4, nz2)
        last = planes2 - 1 - i
        sweep(source, target, weights2, k2, f2, 1 + i, last, mask, origin_x, size_x // 4, AT_ONCE_2)
        source = target
    for j in range(8):
        q2[16 * j : 16 * j + 16, :] = source[4 + j] - v2[4 + j]
    s2[...] = dot_parts(q2[...], shared_matrix(LANES, LANES, 1, 2, 1.0))
    planes1, rows1, nz1 = w1_ref.shape
    d2[...] = jnp.zeros(d2.shape, F32)
    for j in range(8):
        rows = roll(s2[16 * j : 16 * j + 16, :], -4, 0)[:8]
        d2[pl.ds(rows1 * j + 4, 8, 2), :] = rows
        d2[pl.ds(rows1 * j + 5, 8, 2), :] = rows

    own1 = planes1 - 2 * RIM_1
    shape1 = (rows1, nz1)
    weights1 = (wx1, wy1, wz1, wb1, t1)
    origin_x = place_x * own1 - RIM_1
    origin_y = place_y * own1 - RIM_1
    for x in range(4, 20):
        at = rows1 * ((x - 4) // 2)
        a1[x] = w1_ref[x] + d2[at : at + rows1, :]
    mask = row_mask(shape1, 5, rows1 - 5, origin_y, size_y // 2)
    sweep(a1, b1, weights1, k1, f1_ref, 5, planes1 - 5, mask, origin_x, size_x // 2, AT_ONCE_1)
    mask = row_mask(shape1, 6, rows1 - 6, origin_y, size_y // 2)
    sweep(b1, a1, weights1, k1, f1_ref, 6, planes1 - 6, mask, origin_x, size_x // 2, AT_ONCE_1)
    for j in range(12):
        rows = roll(a1[6 + j] - v1_ref[6 + j], -6, 0)[:16]
        d1[pl.ds(32 * j, 16, 2), :] = rows
        d1[pl.ds(32 * j + 1, 16, 2), :] = rows
    nz0 = 2 * nz1
    q0[...] = dot_parts(d1[...], shared_matrix(nz1, nz0, 1, 2, 1.0))

    own_x, own_y = out_ref.shape[:2]
    planes0 = own_x + 2 * RIM_X0
    rows0 = own_y + 2 * RIM_Y0
    shape0 = (rows0, nz0)
    corners = rim_planes(own_x)
    for x in range(planes0):
        if x in corners:
            at = corners.index(x)
            ref, first = (xl_ref, at) if x < RIM_X0 else (xr_ref, at - RIM_X0)
            tiles = [ref[2 * RIM_2 + 4 * first + t] for t in range(4)]
            left, right = cl_ref[4 * RIM_2 + at], cr_ref[4 * RIM_2 + at]
        else:
            tiles = quarter_tiles(u0_ref, x - RIM_X0)
            left, right = yl_ref[8 + x - RIM_X0], yr_ref[8 + x - RIM_X0]
        upper = jnp.concatenate(tiles[:2], axis=1)
        lower = jnp.concatenate(tiles[2:], axis=1)
        left = jnp.where(keep_left, left, 0.0)
        right = jnp.where(keep_right, right, 0.0)
        left = jnp.concatenate([left, roll(left, 4, 0)], axis=1)
        right = jnp.concatenate([roll(right, 4, 0), right], axis=1)
        tiles = shifted_tiles(upper, lower, left, right)
        at = 32 * ((x + 1) // 2)
        for i, tile in enumerate(tiles):
            a0[x, 8 * i : 8 * i + 8, :] = tile + q0[at + 8 * i : at + 8 * i + 8, :]
    weights0 = (wx0, wy0, wz0, wb0, t0)
    origin_x = place_x * own_x - RIM_X0
    origin_y = place_y * own_y - RIM_Y0
    mask = row_mask(shape0, 2, rows0 - 2, origin_y, size_y)
    sweep(a0, b0, weights0, kw_ref, fw_ref, 1, planes0 - 1, mask, origin_x, size_x, AT_ONCE_0)
    mask = row_mask(shape0, 3, rows0 - 3, origin_y, size_y)
    sweep(b0, a0, weights0, kw_ref, fw_ref, 2, planes0 - 2, mask, origin_x, size_x, AT_ONCE_0)
    low = low_half((8, nz0))

    def finish(x, acc):
        d = defect_at(x, a0, weights0, kw_ref, fw_ref[x])
        u = a0[x]
        moved = [roll(u[8 * t : 8 * t + 8], 4, 0) for t in range(3)]
        out_ref[x - RIM_X0, 0:8, :] = jnp.where(low, moved[0], moved[1])
        out_ref[x - RIM_X0, 8:16, :] = jnp.where(low, moved[1], moved[2])
        return acc + d * d

    acc = lax.fori_loop(RIM_X0, RIM_X0 + own_x, finish, jnp.zeros(shape0, F32), unroll=own_x)
    row = iota(shape0, 0)
    acc = jnp.where((row >= RIM_Y0) & (row < RIM_Y0 + own_y), acc, 0.0)
    acc = jnp.sum(acc, axis=0, keepdims=True)
    acc = jnp.sum(acc, axis=1, keepdims=True)
    part_ref[...] = jnp.broadcast_to(acc, part_ref.shape)


def arr(*shape):
    return jax.ShapeDtypeStruct(shape, F32)


def call(kernel, outs, scratch, *args):
    return pl.pallas_call(
        kernel,
        out_shape=outs,
        in_specs=[pl.BlockSpec(memory_space=pltpu.VMEM)] * len(args),
        out_specs=[pl.BlockSpec(memory_space=pltpu.VMEM)] * len(outs),
        scratch_shapes=[pltpu.VMEM(shape, F32) for shape in scratch],
        compiler_params=pltpu.CompilerParams(vmem_limit_bytes=VMEM_LIMIT),
    )(*args)


def swap(upward, downward, axis, ring=False):
    size = lax.axis_size(axis)
    up = [(i, (i + 1) % size) for i in range(size if ring else size - 1)]
    down = [(j, i) for i, j in up]
    return lax.ppermute(upward, axis, up), lax.ppermute(downward, axis, down)


def sum_over(part, axis):
    size = lax.axis_size(axis)
    rows = jnp.broadcast_to(part, (size, LANES))
    return jnp.sum(lax.all_to_all(rows, axis, 0, 0, tiled=True), axis=0, keepdims=True)


def body(start, permit, ion, source):
    own_x, own_y, nz = start.shape
    size_x, size_y = own_x * lax.axis_size("gx"), own_y * lax.axis_size("gy")
    planes0, rows0 = own_x + 2 * RIM_X0, own_y + 2 * RIM_Y0
    window0 = (planes0, rows0, nz)

    fields = (start, permit, ion, source)
    depths = [depth for depth, _ in FINE_SENT]
    upward = jnp.concatenate([a[own_x - d :] for a, d in zip(fields, depths)], axis=0)
    downward = jnp.concatenate([a[:d] for a, d in zip(fields, depths)], axis=0)
    xl, xr = swap(upward, downward, "gx")
    yl, yr = swap(*call(pack_fine_own, [arr(2, own_x, 8, nz)] * 2, [], *fields), "gy", True)
    cl, cr = swap(*call(pack_fine_rim, [arr(2, 2 * RIM_X0, 8, nz)] * 2, [], xl, xr), "gy", True)
    own1, own1_y, nz1 = own_x // 2, own_y // 2, nz // 2
    gathered = 2 * own1 * rows0 + 2 * own1 * own_y
    upward, downward, y_upward, y_downward, stack1, u0, *level0 = call(
        functools.partial(fine_first, size_x=size_x, size_y=size_y),
        [arr(4, own1, own1_y, nz1)] * 5
        + [arr(own_x, own_y, nz)] + [arr(*window0)] * 7,
        [window0] * 3 + [(gathered, nz), (gathered, nz1)],
        *fields, xl, xr, yl, yr, cl, cr,
    )

    xl, xr = swap(upward, downward, "gx")
    yl, yr = swap(y_upward, y_downward, "gy", True)
    rim = arr(4, 2 * (own1 - 1), own1_y, nz1)
    cl, cr = swap(*call(join_rims, [rim, rim], [], xl, xr, yl, yr), "gy", True)
    planes1 = own1 + 2 * RIM_1
    window1 = (planes1, own1_y + 2 * RIM_1, nz1)
    sent_x = 2 * RIM_2 + 4 * RIM_X0
    sent_y = 8 + own_x
    upward, downward, y_upward, y_downward, stack2, *level1 = call(
        functools.partial(middle_first, size_x=size_x // 2, size_y=size_y // 2),
        [arr(sent_x, 8, LANES)] * 2 + [arr(sent_y, 8, LANES)] * 2 + [arr(2, 8, 8, LANES)] + [arr(*window1)] * 9,
        [window1] * 2 + [(16 * window1[1], 2 * nz1), (16 * window1[1], nz1)],
        stack1, xl, xr, yl, yr, cl, cr, u0,
    )

    xl, xr = swap(upward, downward, "gx")
    yl, yr = swap(y_upward, y_downward, "gy", True)
    rim = arr(4 * RIM_2 + 2 * RIM_X0, 8, LANES)
    cl, cr = swap(*call(pack_coarse, [rim, rim], [], xl, xr, yl, yr), "gy", True)
    planes2 = 2 * RIM_2 + 4
    window2 = (planes2, planes2, LANES)
    relaxed, part = call(
        functools.partial(coarse_and_last, size_x=size_x, size_y=size_y),
        [arr(own_x, own_y, nz), arr(8, LANES)],
        [window2] * 10 + [(LANES, LANES)] * 2 + [(8 * window1[1], LANES)]
        + [window1] * 2 + [(12 * 32, nz1)] + [window0] * 2 + [(12 * 32, nz)],
        xl, xr, yl, yr, cl, cr, stack2, u0, *level1, *level0,
    )
    total = sum_over(sum_over(part[:1], "gy"), "gx")[0, 0]
    return relaxed, jnp.sqrt(total / (size_x * size_y * nz))


def solution(mesh):
    specs = (P("gx", "gy", None),) * 4
    return jax.shard_map(
        body, mesh=mesh, in_specs=specs, out_specs=(P("gx", "gy", None), P()), check_vma=False
    )
```
